256 devices in a mesh: seq: 32 (over y, z), head: 8 (over x, core).
Axes of the slice: x: 4, y: 4, z: 8, core: 2. Of those that a mesh axis runs over, the one named last changes fastest.
Arguments:
- queries: bfloat16 [65536, 2048], P('seq', 'head'), may hold values from -2.5 to 2.5
- keys: bfloat16 [65536, 2048], P('seq', 'head'), may hold values from -2.5 to 2.5
- values: bfloat16 [65536, 2048], P('seq', 'head'), may hold values from -2.5 to 2.5
- w_out: bfloat16 [2048, 2048], P('head'), may hold values from -0.125 to 0.125
- grad_out: bfloat16 [65536, 2048], P(('seq', 'head')), may hold values from -6 to 6
Outputs:
- mixed: bfloat16 [65536, 2048], P(('seq', 'head'))
- grad_queries: bfloat16 [65536, 2048], P('seq', 'head')
- grad_keys: bfloat16 [65536, 2048], P('seq', 'head')
- grad_values: bfloat16 [65536, 2048], P('seq', 'head')
- grad_weight: bfloat16 [2048, 2048], P('head')
The draws below stay inside these ranges and needn't reach their ends.
All inputs are finite; a program needn't handle non-finite values.
Results may differ from the reference program's by a relative error of at most 0.013.
Values may be sent and summed in bfloat16 or wider, within the bound.
No kernel may reach another device: no remote copies, remote signals or barrier semaphores. Data moves between devices by JAX's collectives and lax.ppermute only.
A program may use at most 192 MiB of HBM per device.

```python
import math
import jax
import jax.numpy as jnp
from jax import lax

HEADS = 16
HEAD_DIM = 128
B = 128
D = 2048
TOKENS = 65536
LEVELS = 9


def waves(key, amplitude):
    first, second = jax.random.split(key)
    lowest = math.log(2.0 * math.pi * 2.0 / TOKENS)
    highest = math.log(2.0 * math.pi / 32.0)
    freqs = jnp.exp(jax.random.uniform(first, (D,), jnp.float32, lowest, highest))
    phases = jax.random.uniform(second, (D,), jnp.float32, -math.pi, math.pi)
    places = jnp.arange(TOKENS, dtype=jnp.float32)[:, None]
    return amplitude * jnp.cos(places * freqs[None, :] + phases[None, :])


def draw_queries(key, part):
    smooth = waves(key, 0.9)
    key = jax.random.fold_in(key, 3)
    noise = jnp.clip(0.7 * jax.random.normal(key, (TOKENS, D), jnp.float32), -1.5, 1.5)
    return (smooth + noise).astype(jnp.bfloat16)


def draw_keys(key, part):
    smooth = waves(key, 0.9)
    key = jax.random.fold_in(key, 4)
    noise = jnp.clip(0.7 * jax.random.normal(key, (TOKENS, D), jnp.float32), -1.5, 1.5)
    return (smooth + noise).astype(jnp.bfloat16)


def draw_values(key, part):
    key = jax.random.fold_in(key, 5)
    smooth = waves(jax.random.fold_in(key, 1), 1.0)
    noise_key = jax.random.fold_in(key, 2)
    noise = jnp.clip(0.8 * jax.random.normal(noise_key, (TOKENS, D), jnp.float32), -1.5, 1.5)
    return (smooth + noise).astype(jnp.bfloat16)


def steps_of(own_key, shape, cuts, low, high):
    level = 1.0
    for position, shards_of in cuts:
        steps = jax.random.uniform(jax.random.fold_in(jax.random.fold_in(own_key, 6), position), (shards_of,), jnp.float32, low / len(cuts), high / len(cuts))
        level = level * jnp.repeat(jnp.exp(steps), shape[position] // shards_of).reshape((-1,) + (1,) * (len(shape) - 1 - position))
    return level


def bell_draw(own_key, dims, scale, limit, cuts=(), kind=jnp.bfloat16):
    gain = steps_of(own_key, dims, cuts, -0.22, 0.18) if cuts else 1.0
    result = jax.random.normal(own_key, dims, jnp.float32) * scale * gain
    return jnp.minimum(jnp.maximum(result, -limit), limit).astype(kind)


def setup_inputs(seed: int = 0) -> dict:
    key_list = jax.random.split(jax.random.key(seed), 6)
    queries = draw_queries(jax.random.fold_in(key_list[5], 71), 0)
    keys = draw_keys(jax.random.fold_in(key_list[5], 71), 0)
    values = draw_values(jax.random.fold_in(key_list[5], 71), 0)
    w_out = bell_draw(key_list[3], (D, D), D ** -0.5, 0.125, ((0, 8),))
    grad_out = bell_draw(key_list[4], (TOKENS, D), 1.0, 6.0, ((0, 256),))
    return {"queries": queries, "keys": keys, "values": values, "w_out": w_out, "grad_out": grad_out}


def rounded(matrix):
    return lax.optimization_barrier(matrix.astype(jnp.bfloat16)).astype(jnp.float32)


def pair_mean(matrix):
    pairs = matrix.reshape(matrix.shape[0] // 2, 2, matrix.shape[1]).astype(jnp.float32)
    return ((pairs[:, 0] + pairs[:, 1]) * 0.5).astype(jnp.bfloat16)


def pair_sum(matrix):
    pairs = matrix.reshape((matrix.shape[0] // 2, 2) + matrix.shape[1:])
    return pairs[:, 0] + pairs[:, 1]


def swap_blocks(blocks):
    dims_in = blocks.shape
    return blocks.reshape((dims_in[0] // 2, 2) + dims_in[1:])[:, ::-1].reshape(dims_in)


def spread(matrix, repeats):
    dims_in = matrix.shape
    widened = jnp.broadcast_to(matrix[:, None], (dims_in[0], repeats) + dims_in[1:])
    return widened.reshape((dims_in[0] * repeats,) + dims_in[1:])


def coarse_levels(matrix):
    stack_list = [matrix]
    for level in range(1, LEVELS):
        stack_list.append(pair_mean(stack_list[-1]))
    return stack_list


def head_forward(operands):
    queries, keys, values = operands
    scale = HEAD_DIM ** -0.5
    q_levels = coarse_levels(queries)
    k_levels = coarse_levels(keys)
    v_levels = coarse_levels(values)
    numer = jnp.zeros((TOKENS, HEAD_DIM), jnp.float32)
    total = jnp.zeros((TOKENS,), jnp.float32)
    for level in range(LEVELS):
        weight = 2.0 ** level
        blocks = TOKENS // (2 ** level) // B
        query_blocks = q_levels[level].reshape(blocks, B, HEAD_DIM).astype(jnp.float32)
        key_blocks = k_levels[level].reshape(blocks, B, HEAD_DIM).astype(jnp.float32)
        value_blocks = v_levels[level].reshape(blocks, B, HEAD_DIM).astype(jnp.float32)
        pairings = [(swap_blocks(key_blocks), swap_blocks(value_blocks))]
        if level == 0:
            pairings.append((key_blocks, value_blocks))
        for key_side, value_side in pairings:
            expos = jnp.exp(jnp.einsum("nqd,nkd->nqk", query_blocks, key_side) * scale)
            total = total + spread((weight * jnp.sum(expos, axis=-1)).reshape(-1), 2 ** level)
            level_numer = weight * jnp.einsum("nqk,nkd->nqd", rounded(expos), value_side)
            numer = numer + spread(level_numer.reshape(-1, HEAD_DIM), 2 ** level)
    return (numer / total[:, None]).astype(jnp.bfloat16), total


def head_backward(operands):
    queries, keys, values, attended, grad_attended, total = operands
    scale = HEAD_DIM ** -0.5
    q_levels = coarse_levels(queries)
    k_levels = coarse_levels(keys)
    v_levels = coarse_levels(values)
    g_levels = [grad_attended / total[:, None]]
    h_levels = [jnp.sum(grad_attended * attended.astype(jnp.float32), axis=-1) / total]
    for level in range(1, LEVELS):
        g_levels.append(pair_sum(g_levels[-1]))
        h_levels.append(pair_sum(h_levels[-1]))
    grad_q = jnp.zeros((TOKENS, HEAD_DIM), jnp.float32)
    grad_k = jnp.zeros((TOKENS, HEAD_DIM), jnp.float32)
    grad_v = jnp.zeros((TOKENS, HEAD_DIM), jnp.float32)
    for level in range(LEVELS):
        weight = 2.0 ** level
        blocks = TOKENS // (2 ** level) // B
        query_blocks = q_levels[level].reshape(blocks, B, HEAD_DIM).astype(jnp.float32)
        key_blocks = k_levels[level].reshape(blocks, B, HEAD_DIM).astype(jnp.float32)
        value_blocks = v_levels[level].reshape(blocks, B, HEAD_DIM).astype(jnp.float32)
        grad_blocks = rounded(g_levels[level]).reshape(blocks, B, HEAD_DIM)
        dot_blocks = h_levels[level].reshape(blocks, B)
        pairings = [(swap_blocks(key_blocks), swap_blocks(value_blocks), True)]
        if level == 0:
            pairings.append((key_blocks, value_blocks, False))
        for key_side, value_side, swapped in pairings:
            expos = jnp.exp(jnp.einsum("nqd,nkd->nqk", query_blocks, key_side) * scale)
            probe = jnp.einsum("nqd,nkd->nqk", grad_blocks, value_side)
            slopes = rounded(weight * expos * (probe - dot_blocks[..., None]))
            level_q = scale * jnp.einsum("nqk,nkd->nqd", slopes, key_side)
            level_k = scale * jnp.einsum("nqk,nqd->nkd", slopes, query_blocks)
            level_v = weight * jnp.einsum("nqk,nqd->nkd", rounded(expos), grad_blocks)
            if swapped:
                level_k = swap_blocks(level_k)
                level_v = swap_blocks(level_v)
            grad_q = grad_q + spread(level_q.reshape(-1, HEAD_DIM), 2 ** level) / weight
            grad_k = grad_k + spread(level_k.reshape(-1, HEAD_DIM), 2 ** level) / weight
            grad_v = grad_v + spread(level_v.reshape(-1, HEAD_DIM), 2 ** level) / weight
    return grad_q.astype(jnp.bfloat16), grad_k.astype(jnp.bfloat16), grad_v.astype(jnp.bfloat16)


def by_head(matrix):
    return jnp.transpose(matrix.reshape(TOKENS, HEADS, HEAD_DIM), (1, 0, 2))


def by_token(stacked):
    return jnp.transpose(stacked, (1, 0, 2)).reshape(TOKENS, HEADS * HEAD_DIM)


def reference(queries, keys, values, w_out, grad_out):
    heads_q = by_head(queries)
    heads_k = by_head(keys)
    heads_v = by_head(values)
    attended_heads, totals = lax.map(head_forward, (heads_q, heads_k, heads_v))
    attended = by_token(attended_heads)
    mixed = jnp.dot(attended, w_out, preferred_element_type=jnp.float32).astype(jnp.bfloat16)
    grad_weight = jnp.dot(attended.T, grad_out, preferred_element_type=jnp.float32).astype(jnp.bfloat16)
    grad_attended = jnp.dot(grad_out, w_out.T, preferred_element_type=jnp.float32)
    grads = lax.map(head_backward, (heads_q, heads_k, heads_v, attended_heads, by_head(grad_attended), totals))
    return mixed, by_token(grads[0]), by_token(grads[1]), by_token(grads[2]), grad_weight
```

```python
import functools
import jax
import jax.numpy as jnp
from jax import lax
from jax.experimental import pallas as pl
from jax.experimental.pallas import tpu as pltpu
from jax.sharding import PartitionSpec as P

HD = 128
B = 128
LOCAL = 4
F32 = jnp.float32
BF16 = jnp.bfloat16
EXP_SCALE = 1.4426950408889634 * HD ** (-0.5)
SCALE = HD ** (-0.5)
VMEM = 56 * 1024 * 1024


def nn(a, b):
    return lax.dot_general(a, b, (((1,), (0,)), ((), ())), preferred_element_type=F32)


def nt(a, b):
    return lax.dot_general(a, b, (((1,), (1,)), ((), ())), preferred_element_type=F32)


def tn(a, b):
    return lax.dot_general(a, b, (((0,), (0,)), ((), ())), preferred_element_type=F32)


def params():
    return pltpu.CompilerParams(vmem_limit_bytes=VMEM)


def offset(level, tokens):
    return tokens - (tokens >> (level - 1))


def spec(rows, block=0):
    return pl.BlockSpec((rows, HD), lambda h: (block, h))


def lead(rows, width):
    return pl.BlockSpec((1, rows, width), lambda h: (h, 0, 0))


def with_ones(v):
    return jnp.concatenate([v, jnp.ones(v.shape, BF16)], axis=1)


def repeat2(x, scratch, base=0):
    n = x.shape[0]
    scratch[pl.ds(base, n, stride=2), :] = x
    scratch[pl.ds(base + 1, n, stride=2), :] = x


def coarsen_kernel(q_ref, k_ref, v_ref, qc_ref, kc_ref, vc_ref):
    tokens = q_ref.shape[0]
    r = lax.broadcasted_iota(jnp.int32, (B, 2 * B), 0)
    c = lax.broadcasted_iota(jnp.int32, (B, 2 * B), 1)
    mean = jnp.where(c // 2 == r, 0.5, 0.0).astype(BF16)
    half = mean[:64, :128]
    for src, dst in ((q_ref, qc_ref), (k_ref, kc_ref), (v_ref, vc_ref)):
        for i in range(tokens // 256):
            dst[i * B:(i + 1) * B, :] = nn(mean, src[i * 256:(i + 1) * 256, :]).astype(BF16)
    for level in range(2, LOCAL + 1):
        before, here = offset(level - 1, tokens), offset(level, tokens)
        for dst in (qc_ref, kc_ref, vc_ref):
            for i in range((tokens >> level) // B):
                rows = dst[before + i * 256:before + (i + 1) * 256, :]
                dst[here + i * B:here + (i + 1) * B, :] = nn(mean, rows).astype(BF16)
    tail = offset(LOCAL + 1, tokens)
    for dst in (qc_ref, kc_ref, vc_ref):
        x5 = nn(half, dst[tail - B:tail, :]).astype(BF16)
        x6 = nn(half[:32, :64], x5).astype(BF16)
        x7 = nn(half[:16, :32], x6).astype(BF16)
        x8 = nn(half[:16, :16], x7).astype(BF16)
        dst[tail:tail + 64, :] = x5
        dst[tail + 64:tail + 96, :] = x6
        dst[tail + 96:tail + 112, :] = x7
        dst[tail + 112:tail + 128, :] = x8


def coarsen(q, k, v):
    shape = jax.ShapeDtypeStruct(q.shape, BF16)
    tokens = q.shape[0]
    return pl.pallas_call(
        coarsen_kernel,
        grid=(q.shape[1] // HD,),
        in_specs=[spec(tokens)] * 3,
        out_specs=[spec(tokens)] * 3,
        out_shape=[shape] * 3,
        compiler_params=params(),
        name="coarsen",
    )(q, k, v)


def forward_block(q, k, v):
    expos = jnp.exp2(nt(q, k) * EXP_SCALE).astype(BF16)
    return nn(expos, with_ones(v))


def local_forward_kernel(q_ref, k_ref, v_ref, qc_ref, kc_ref, vc_ref, numer_ref, total_ref, *scr):
    tokens = q_ref.shape[0]
    for level in range(LOCAL - 1, 0, -1):
        off = offset(level, tokens)
        for i in range((tokens >> level) // 256):
            at = off + i * 256
            lo, hi = slice(at, at + B), slice(at + B, at + 256)
            for j, (mine, other) in enumerate(((lo, hi), (hi, lo))):
                u = forward_block(qc_ref[mine, :], kc_ref[other, :], vc_ref[other, :])
                n, t = u[:, :HD], u[:, HD:]
                rows = slice(i * 256 + j * B, i * 256 + (j + 1) * B)
                if level < LOCAL - 1:
                    n = n + 2.0 * scr[2 * level][rows, :]
                    t = t + 2.0 * scr[2 * level + 1][rows, :]
                repeat2(n, scr[2 * level - 2], 2 * rows.start)
                repeat2(t, scr[2 * level - 1], 2 * rows.start)
    for i in range(tokens // 256):
        rows = slice(i * 256, (i + 1) * 256)
        u = forward_block(q_ref[rows, :], k_ref[rows, :], v_ref[rows, :])
        numer_ref[0, rows, :] = u[:, :HD] + 2.0 * scr[0][rows, :]
        total_ref[0, rows, :] = u[:, HD:] + 2.0 * scr[1][rows, :]


def local_forward(q, k, v, qc, kc, vc):
    tokens, width = q.shape
    heads = width // HD
    scratch = []
    for level in range(1, LOCAL):
        scratch += [pltpu.VMEM((tokens >> (level - 1), HD), F32)] * 2
    shape = jax.ShapeDtypeStruct((heads, tokens, HD), F32)
    return pl.pallas_call(
        local_forward_kernel,
        grid=(heads,),
        in_specs=[spec(tokens)] * 6,
        out_specs=[lead(tokens, HD)] * 2,
        out_shape=[shape] * 2,
        scratch_shapes=scratch,
        compiler_params=params(),
        name="local_forward",
    )(q, k, v, qc, kc, vc)


def level_of_row(row):
    steps = [(row >= edge).astype(jnp.int32) for edge in (128, 192, 224, 240, 248)]
    return sum(steps)


def spread_levels(packed, scratch, weight):
    bounds = (0, 128, 192, 224, 240, 248)
    x = packed[240:248, :]
    for i in range(3, -1, -1):
        lo, hi = bounds[i], bounds[i + 1]
        repeat2(x, scratch)
        x = packed[lo:hi, :] + weight * scratch[0:hi - lo, :]
    return x


def repeat16(x, scratch):
    n = x.shape[0]
    for j in range(16):
        scratch[pl.ds(j, n, stride=16), :] = x


def coarse_forward_kernel(numer_ref, total_ref, q_ref, k_ref, v_ref, att_ref, rtot_ref, small, big_n, big_t):
    rows, keys = q_ref.shape[0], k_ref.shape[0]
    level = level_of_row(lax.broadcasted_iota(jnp.int32, (rows, keys), 0))
    group = lax.broadcasted_iota(jnp.int32, (rows, keys), 1) // B
    expos = jnp.where(level == group, jnp.exp2(nt(q_ref[...], k_ref[...]) * EXP_SCALE), 0.0)
    u = nn(expos.astype(BF16), with_ones(v_ref[...]))
    repeat16(16.0 * spread_levels(u[:, :HD], small, 2.0), big_n)
    repeat16(16.0 * spread_levels(u[:, HD:], small, 2.0), big_t)
    rtot = 1.0 / (total_ref[0] + big_t[...])
    rtot_ref[0] = rtot
    att_ref[...] = ((numer_ref[0] + big_n[...]) * rtot).astype(BF16)


def coarse_forward(numer, total, qc, kall, vall):
    heads, tokens, _ = numer.shape
    keys = kall.shape[0]
    return pl.pallas_call(
        coarse_forward_kernel,
        grid=(heads,),
        in_specs=[lead(tokens, HD)] * 2 + [spec(256, tokens // 256 - 1)] + [spec(keys)] * 2,
        out_specs=[spec(tokens), lead(tokens, HD)],
        out_shape=[
            jax.ShapeDtypeStruct((tokens, heads * HD), BF16),
            jax.ShapeDtypeStruct((heads, tokens, HD), F32),
        ],
        scratch_shapes=[pltpu.VMEM((B, HD), F32)] + [pltpu.VMEM((tokens, HD), F32)] * 2,
        compiler_params=params(),
        name="coarse_forward",
    )(numer, total, qc, kall, vall)


def with_dot(g, dot):
    lane = lax.broadcasted_iota(jnp.int32, dot.shape, 1)
    high = (-dot).astype(BF16)
    low = (-dot - high.astype(F32)).astype(BF16)
    zero = jnp.zeros(dot.shape, BF16)
    parts = jnp.where(lane == 0, high, jnp.where(lane == 1, low, zero))
    return jnp.concatenate([g.astype(BF16), parts], axis=1)


def backward_block(q, k, v, g, mask=None):
    expos = jnp.exp2(nt(k, q) * EXP_SCALE)
    if mask is not None:
        expos = jnp.where(mask, expos, 0.0)
    slopes = (expos * nt(with_ones(v), g)).astype(BF16)
    dq = tn(slopes, k)
    dk = nn(slopes, q)
    dv = nn(expos.astype(BF16), g[:, :HD])
    return dq, dk, dv


def coarse_backward_kernel(
    ga_ref, att_ref, rtot_ref, q_ref, k_ref, v_ref, g0_ref, gc_ref, dq_ref, dk_ref, dv_ref, g_scr, d_scr, small
):
    tokens = ga_ref.shape[0]
    step = 256
    for i in range(tokens // step):
        rows = slice(i * step, (i + 1) * step)
        ga = ga_ref[rows, :].astype(F32)
        rtot = rtot_ref[0, rows, :]
        g = ga * rtot
        dot = jnp.sum(ga * att_ref[rows, :].astype(F32), axis=1, keepdims=True) * rtot
        g_scr[rows, :] = g
        d_scr[rows, :] = dot
        g0_ref[0, rows, :] = with_dot(g, dot)
    for level in range(1, 9):
        n = tokens >> level
        here = offset(level, tokens)
        chunk = min(n, 256)
        for i in range(n // chunk):
            even, odd = pl.ds(2 * i * chunk, chunk, stride=2), pl.ds(2 * i * chunk + 1, chunk, stride=2)
            g = g_scr[even, :] + g_scr[odd, :]
            dot = d_scr[even, :] + d_scr[odd, :]
            g_scr[i * chunk:(i + 1) * chunk, :] = g
            d_scr[i * chunk:(i + 1) * chunk, :] = dot
            if n < 16:
                pad = jnp.zeros((16 - n, HD), F32)
                g, dot = jnp.concatenate([g, pad], axis=0), jnp.concatenate([dot, pad], axis=0)
            gc_ref[0, here + i * chunk:here + i * chunk + g.shape[0], :] = with_dot(g, dot)
    rows, keys = q_ref.shape[0], k_ref.shape[0]
    level = level_of_row(lax.broadcasted_iota(jnp.int32, (keys, rows), 1))
    group = lax.broadcasted_iota(jnp.int32, (keys, rows), 0) // B
    g = gc_ref[0, tokens - rows:tokens, :]
    dq, dk, dv = backward_block(q_ref[...], k_ref[...], v_ref[...], g, level == group)
    dq_ref[0] = spread_levels(dq, small, 1.0)
    dk_ref[...] = (dk * SCALE).astype(BF16)
    dv_ref[...] = dv.astype(BF16)


def coarse_backward(ga, att, rtot, qc, kall, vall):
    heads, tokens, _ = rtot.shape
    keys = kall.shape[0]
    wide = jax.ShapeDtypeStruct((heads, tokens, 2 * HD), BF16)
    side = jax.ShapeDtypeStruct((keys, heads * HD), BF16)
    return pl.pallas_call(
        coarse_backward_kernel,
        grid=(heads,),
        in_specs=[spec(tokens)] * 2 + [lead(tokens, HD), spec(256, tokens // 256 - 1)] + [spec(keys)] * 2,
        out_specs=[lead(tokens, 2 * HD)] * 2 + [lead(B, HD)] + [spec(keys)] * 2,
        out_shape=[wide, wide, jax.ShapeDtypeStruct((heads, B, HD), F32), side, side],
        scratch_shapes=[pltpu.VMEM((tokens, HD), F32)] * 2 + [pltpu.VMEM((B, HD), F32)],
        compiler_params=params(),
        name="coarse_backward",
    )(ga, att, rtot, qc, kall, vall)


def local_backward_kernel(
    q_ref, k_ref, v_ref, qc_ref, kc_ref, vc_ref, g0_ref, gc_ref, dq4_ref, dq_ref, dk_ref, dv_ref, *scr
):
    tokens = q_ref.shape[0]
    for level in range(LOCAL - 1, 0, -1):
        off = offset(level, tokens)
        sq, sk, sv = scr[3 * level - 3:3 * level]
        if level == LOCAL - 1:
            repeat2(dq4_ref[0], scr[3 * level])
        uq = scr[3 * level]
        uk, uv = scr[3 * level + 1:3 * level + 3] if level < LOCAL - 1 else (None, None)
        for i in range((tokens >> level) // 256):
            at = off + i * 256
            lo, hi = (at, i * 256), (at + B, i * 256 + B)
            for (ma, mr), (oa, orow) in ((lo, hi), (hi, lo)):
                mine, other = slice(ma, ma + B), slice(oa, oa + B)
                dq, dk, dv = backward_block(qc_ref[mine, :], kc_ref[other, :], vc_ref[other, :], gc_ref[0, mine, :])
                dq = dq + uq[mr:mr + B, :]
                if uk is not None:
                    dk = dk + uk[orow:orow + B, :]
                    dv = dv + uv[orow:orow + B, :]
                repeat2(dq, sq, 2 * mr)
                repeat2(dk, sk, 2 * orow)
                repeat2(dv, sv, 2 * orow)
    for i in range(tokens // 256):
        rows = slice(i * 256, (i + 1) * 256)
        dq, dk, dv = backward_block(q_ref[rows, :], k_ref[rows, :], v_ref[rows, :], g0_ref[0, rows, :])
        dq_ref[rows, :] = ((dq + scr[0][rows, :]) * SCALE).astype(BF16)
        dk_ref[rows, :] = ((dk + scr[1][rows, :]) * SCALE).astype(BF16)
        dv_ref[rows, :] = (dv + scr[2][rows, :]).astype(BF16)


def local_backward(q, k, v, qc, kc, vc, g0, gc, dq4):
    tokens, width = q.shape
    heads = width // HD
    scratch = []
    for level in range(1, LOCAL):
        scratch += [pltpu.VMEM((tokens >> (level - 1), HD), F32)] * 3
    scratch += [pltpu.VMEM((tokens >> (LOCAL - 1), HD), F32)]
    shape = jax.ShapeDtypeStruct((tokens, width), BF16)
    return pl.pallas_call(
        local_backward_kernel,
        grid=(heads,),
        in_specs=[spec(tokens)] * 6 + [lead(tokens, 2 * HD)] * 2 + [lead(B, HD)],
        out_specs=[spec(tokens)] * 3,
        out_shape=[shape] * 3,
        scratch_shapes=scratch,
        compiler_params=params(),
        name="local_backward",
    )(q, k, v, qc, kc, vc, g0, gc, dq4)


def finish_kernel(dk_ref, dv_ref, ck_ref, cv_ref, gk_ref, gv_ref, small, big):
    for part, coarse, out in ((dk_ref, ck_ref, gk_ref), (dv_ref, cv_ref, gv_ref)):
        repeat16(spread_levels(coarse[...].astype(F32), small, 1.0), big)
        out[...] = (part[...].astype(F32) + big[...]).astype(BF16)


def finish(dk, dv, ck, cv):
    tokens, width = dk.shape
    shape = jax.ShapeDtypeStruct((tokens, width), BF16)
    return pl.pallas_call(
        finish_kernel,
        grid=(width // HD,),
        in_specs=[spec(tokens)] * 2 + [spec(256)] * 2,
        out_specs=[spec(tokens)] * 2,
        out_shape=[shape] * 2,
        scratch_shapes=[pltpu.VMEM((B, HD), F32), pltpu.VMEM((tokens, HD), F32)],
        compiler_params=params(),
        name="finish",
    )(dk, dv, ck, cv)


def swap(x, axis, distance):
    return lax.ppermute(x, axis, [(i, i ^ distance) for i in range(lax.axis_size(axis))])


ROWS = (128, 64, 32, 16, 8)
START = (0, 128, 192, 224, 240)


def cat(parts):
    return jnp.concatenate(parts, axis=0) if len(parts) > 1 else parts[0]


def gather_siblings(packed, count):
    groups = {i: packed[START[i]:START[i] + ROWS[i]] for i in range(count)}
    found = {}
    for b in range(0, count, 2):
        pair = b + 1 < count
        later = [i for i in range(b + 2, count)]
        common = [groups[i] for i in later]
        arrived = {}
        sent = {1: [groups[b]] + common}
        if pair:
            sent[2] = sent[3] = [groups[b + 1]] + common
        for j, parts in sent.items():
            arrived[j] = swap(cat(parts), "seq", j << b)
        found[b] = arrived[1][:B]
        if pair:
            found[b + 1] = cat([arrived[2][:64], arrived[3][:64]])
            lead = {1: B, 2: 64, 3: 64}
            for i in later:
                n = groups[i].shape[0]
                pieces = [groups[i]] + [arrived[j][lead[j]:lead[j] + n] for j in (1, 2, 3)]
                lead = {j: at + n for j, at in lead.items()}
                groups[i] = cat(pieces)
    return cat([found[i] for i in range(count)])


def return_siblings(partial, count):
    parts = {i: partial[i * B:(i + 1) * B] for i in range(count)}
    for b in range((count - 1) // 2 * 2, -1, -2):
        pair = b + 1 < count
        later = [i for i in range(b + 2, count)]
        quarter = {i: parts[i].shape[0] // 4 for i in later}
        cut = lambda i, j: parts[i][j * quarter[i]:(j + 1) * quarter[i]]
        sent = {1: [parts[b]] + [cut(i, 1) for i in later]}
        if pair:
            sent[2] = [parts[b + 1][:64]] + [cut(i, 2) for i in later]
            sent[3] = [parts[b + 1][64:]] + [cut(i, 3) for i in later]
        arrived = {j: swap(cat(x), "seq", j << b) for j, x in sent.items()}
        parts[b] = arrived[1][:B]
        if pair:
            parts[b + 1] = arrived[2][:64] + arrived[3][:64]
            lead = {1: B, 2: 64, 3: 64}
            for i in later:
                n = quarter[i]
                total = cut(i, 0).astype(F32)
                for j in (1, 2, 3):
                    total = total + arrived[j][lead[j]:lead[j] + n].astype(F32)
                lead = {j: at + n for j, at in lead.items()}
                parts[i] = total.astype(BF16)
    pad = jnp.zeros((256 - sum(ROWS[:count]), partial.shape[1]), partial.dtype)
    return cat([parts[i] for i in range(count)] + [pad])


def sum_over_sequence(x, count):
    low = max(count - 2, 0)
    n = x.shape[0] // 4
    high = lax.axis_index("seq") >> low
    if count < 2:
        for b in range(count):
            x = x + swap(x, "seq", 1 << b)
        return x.astype(BF16)
    pieces = lambda j: lax.dynamic_slice_in_dim(x, (high ^ j) * n, n, 0)
    arrived = [swap(pieces(j).astype(BF16), "seq", j << low) for j in (1, 2, 3)]
    total = pieces(0) + sum(y.astype(F32) for y in arrived)
    for b in range(low):
        mine = total.astype(BF16)
        total = total + swap(mine, "seq", 1 << b).astype(F32)
    mine = total.astype(BF16)
    whole = jnp.zeros(x.shape, BF16)
    for j, y in enumerate([mine] + [swap(mine, "seq", j << low) for j in (1, 2, 3)]):
        whole = lax.dynamic_update_slice_in_dim(whole, y, (high ^ j) * n, 0)
    return whole


def body(queries, keys, values, w_out, grad_out):
    tokens, width = queries.shape
    shards = lax.axis_size("head")
    count = lax.axis_size("seq").bit_length() - 1
    cotangent = lax.all_gather(grad_out, "head", axis=0, tiled=True)
    w_full = lax.all_gather(w_out, "head", axis=0, tiled=True)
    qc, kc, vc = coarsen(queries, keys, values)
    packed = jnp.concatenate([kc[tokens - 256:], vc[tokens - 256:]], axis=1)
    siblings = gather_siblings(packed, count)
    kall, vall = siblings[:, :width], siblings[:, width:]
    numer, total = local_forward(queries, keys, values, qc, kc, vc)
    attended, rtot = coarse_forward(numer, total, qc, kall, vall)

    mine = lax.all_to_all(attended.reshape(shards, tokens // shards, width), "head", 0, 0)
    mine = jnp.transpose(mine, (1, 0, 2)).reshape(tokens // shards, shards * width)
    mixed = jnp.dot(mine, w_full, preferred_element_type=F32).astype(BF16)
    ga = nt(cotangent, w_out)
    grad_weight = sum_over_sequence(tn(attended, cotangent), count)

    g0, gc, dq4, dk_side, dv_side = coarse_backward(ga, attended, rtot, qc, kall, vall)
    returned = return_siblings(jnp.concatenate([dk_side, dv_side], axis=1), count)
    grad_q, dk, dv = local_backward(queries, keys, values, qc, kc, vc, g0, gc, dq4)
    grad_k, grad_v = finish(dk, dv, returned[:, :width], returned[:, width:])
    return mixed, grad_q, grad_k, grad_v, grad_weight


def solution(mesh):
    return jax.shard_map(
        body,
        mesh=mesh,
        in_specs=(
            P("seq", "head"),
            P("seq", "head"),
            P("seq", "head"),
            P("head", None),
            P(("seq", "head"), None),
        ),
        out_specs=(
            P(("seq", "head"), None),
            P("seq", "head"),
            P("seq", "head"),
            P("seq", "head"),
            P("head", None),
        ),
        check_vma=False,
    )
```

```python
import functools
import jax
import jax.numpy as jnp
from jax import lax
from jax.experimental import pallas as pl
from jax.experimental.pallas import tpu as pltpu
from jax.sharding import PartitionSpec as P

HD = 128
B = 128
LOCAL = 4
F32 = jnp.float32
BF16 = jnp.bfloat16
EXP_SCALE = 1.4426950408889634 * HD ** (-0.5)
SCALE = HD ** (-0.5)
VMEM = 56 * 1024 * 1024
COST = 0.05e6


def nn(a, b):
    return lax.dot_general(a, b, (((1,), (0,)), ((), ())), preferred_element_type=F32)


def nt(a, b):
    return lax.dot_general(a, b, (((1,), (1,)), ((), ())), preferred_element_type=F32)


def tn(a, b):
    return lax.dot_general(a, b, (((0,), (0,)), ((), ())), preferred_element_type=F32)


def call(kernel, micros, **kwargs):
    cost = pl.CostEstimate(flops=0, bytes_accessed=int(micros * COST), transcendentals=0)
    return pl.pallas_call(
        kernel,
        cost_estimate=cost,
        compiler_params=pltpu.CompilerParams(vmem_limit_bytes=VMEM),
        **kwargs,
    )


def offset(level, tokens):
    return tokens - (tokens >> (level - 1))


def spec(rows, block=0):
    return pl.BlockSpec((rows, HD), lambda h: (block, h))


def lead(rows, width):
    return pl.BlockSpec((1, rows, width), lambda h: (h, 0, 0))


def both(rows):
    return pl.BlockSpec((rows, 2 * HD), lambda h: (0, h))


def with_ones(v):
    return jnp.concatenate([v, jnp.ones(v.shape, BF16)], axis=1)


def repeat2(x, scratch, base=0):
    n = x.shape[0]
    scratch[pl.ds(base, n, stride=2), :] = x
    scratch[pl.ds(base + 1, n, stride=2), :] = x


def coarsen_kernel(q_ref, k_ref, v_ref, qc_ref, kc_ref, vc_ref, m1_ref, m2_ref):
    tokens = q_ref.shape[0]
    r = lax.broadcasted_iota(jnp.int32, (B, 2 * B), 0)
    c = lax.broadcasted_iota(jnp.int32, (B, 2 * B), 1)
    mean = jnp.where(c // 2 == r, 0.5, 0.0).astype(BF16)
    half = mean[:64, :128]
    for src, dst in ((q_ref, qc_ref), (k_ref, kc_ref), (v_ref, vc_ref)):
        for i in range(tokens // 256):
            dst[i * B:(i + 1) * B, :] = nn(mean, src[i * 256:(i + 1) * 256, :]).astype(BF16)
    for level in range(2, LOCAL + 1):
        before, here = offset(level - 1, tokens), offset(level, tokens)
        for dst in (qc_ref, kc_ref, vc_ref):
            for i in range((tokens >> level) // B):
                rows = dst[before + i * 256:before + (i + 1) * 256, :]
                dst[here + i * B:here + (i + 1) * B, :] = nn(mean, rows).astype(BF16)
    tail = offset(LOCAL + 1, tokens)
    for dst in (qc_ref, kc_ref, vc_ref):
        x5 = nn(half, dst[tail - B:tail, :]).astype(BF16)
        x6 = nn(half[:32, :64], x5).astype(BF16)
        x7 = nn(half[:16, :32], x6).astype(BF16)
        x8 = nn(half[:16, :16], x7).astype(BF16)
        dst[tail:tail + 64, :] = x5
        dst[tail + 64:tail + 96, :] = x6
        dst[tail + 96:tail + 112, :] = x7
        dst[tail + 112:tail + 128, :] = x8
    tail = tokens - 64
    for lane, src in ((0, kc_ref), (HD, vc_ref)):
        columns = slice(lane, lane + HD)
        m1_ref[:B, columns] = src[tokens - 256:tokens - 128, :]
        m2_ref[:64, columns] = src[tokens - 128:tail, :]
        m1_ref[B:, columns] = src[tail:, :]
        m2_ref[64:, columns] = src[tail:, :]


def coarsen(q, k, v):
    shape = jax.ShapeDtypeStruct(q.shape, BF16)
    tokens, width = q.shape
    sizes = (192, 128)
    return call(
        coarsen_kernel,
        6,
        grid=(width // HD,),
        in_specs=[spec(tokens)] * 3,
        out_specs=[spec(tokens)] * 3 + [both(n) for n in sizes],
        out_shape=[shape] * 3 + [jax.ShapeDtypeStruct((n, 2 * width), BF16) for n in sizes],
        name="coarsen",
    )(q, k, v)


def forward_block(q, k, v):
    expos = jnp.exp2(nt(q, k) * EXP_SCALE).astype(BF16)
    return nn(expos, with_ones(v))


def local_forward_kernel(q_ref, k_ref, v_ref, qc_ref, kc_ref, vc_ref, numer_ref, total_ref, *scr):
    tokens = q_ref.shape[0]
    for level in range(LOCAL - 1, 0, -1):
        off = offset(level, tokens)
        for i in range((tokens >> level) // 256):
            at = off + i * 256
            lo, hi = slice(at, at + B), slice(at + B, at + 256)
            for j, (mine, other) in enumerate(((lo, hi), (hi, lo))):
                u = forward_block(qc_ref[mine, :], kc_ref[other, :], vc_ref[other, :])
                n, t = u[:, :HD], u[:, HD:]
                rows = slice(i * 256 + j * B, i * 256 + (j + 1) * B)
                if level < LOCAL - 1:
                    n = n + 2.0 * scr[2 * level][rows, :]
                    t = t + 2.0 * scr[2 * level + 1][rows, :]
                repeat2(n, scr[2 * level - 2], 2 * rows.start)
                repeat2(t, scr[2 * level - 1], 2 * rows.start)
    for i in range(tokens // 256):
        rows = slice(i * 256, (i + 1) * 256)
        u = forward_block(q_ref[rows, :], k_ref[rows, :], v_ref[rows, :])
        numer_ref[0, rows, :] = u[:, :HD] + 2.0 * scr[0][rows, :]
        total_ref[0, rows, :] = u[:, HD:] + 2.0 * scr[1][rows, :]


def local_forward(head, q, k, v, qc, kc, vc):
    tokens, width = q.shape
    scratch = []
    for level in range(1, LOCAL):
        scratch += [pltpu.VMEM((tokens >> (level - 1), HD), F32)] * 2
    columns = pl.BlockSpec((tokens, HD), lambda i: (0, head))
    return call(
        local_forward_kernel,
        5,
        grid=(1,),
        in_specs=[columns] * 6,
        out_specs=[lead(tokens, HD)] * 2,
        out_shape=[jax.ShapeDtypeStruct((1, tokens, HD), F32)] * 2,
        scratch_shapes=scratch,
        name="local_forward",
    )(q, k, v, qc, kc, vc)


def level_of_row(row):
    steps = [(row >= edge).astype(jnp.int32) for edge in (128, 192, 224, 240, 248)]
    return sum(steps)


KEYS = 640
ARRIVED = (192, 128, 128, 160, 96, 96, 128)
USED = (128, 64, 64, 128, 64, 64, 128)


def spread_levels(packed, scratch, weight):
    bounds = (0, 128, 192, 224, 240, 248)
    x = packed[240:248, :]
    for i in range(3, -1, -1):
        lo, hi = bounds[i], bounds[i + 1]
        repeat2(x, scratch)
        x = packed[lo:hi, :] + weight * scratch[0:hi - lo, :]
    return x


def repeat16(x, scratch):
    n = x.shape[0]
    for j in range(16):
        scratch[pl.ds(j, n, stride=16), :] = x


def coarse_forward_kernel(numer0, total0, numer1, total1, q_ref, *refs):
    arrived, (att_ref, rtot_ref, side_ref, small, big_n, big_t) = refs[:7], refs[7:]
    at = 0
    for ref, n in zip(arrived, USED):
        side_ref[at:at + n, :] = ref[:n, :]
        at += n
    rows = q_ref.shape[0]
    level = level_of_row(lax.broadcasted_iota(jnp.int32, (rows, KEYS), 0))
    other = lax.broadcasted_iota(jnp.int32, (rows, KEYS), 1) // B
    expos = jnp.where(level == other, jnp.exp2(nt(q_ref[...], side_ref[:, :HD]) * EXP_SCALE), 0.0)
    u = nn(expos.astype(BF16), with_ones(side_ref[:, HD:]))
    repeat16(16.0 * spread_levels(u[:, :HD], small, 2.0), big_n)
    repeat16(16.0 * spread_levels(u[:, HD:], small, 2.0), big_t)
    for head, numer_ref, total_ref in ((0, numer0, total0), (1, numer1, total1)):

        @pl.when(pl.program_id(0) == head)
        def _():
            rtot = 1.0 / (total_ref[0] + big_t[...])
            rtot_ref[0] = rtot
            att_ref[...] = ((numer_ref[0] + big_n[...]) * rtot).astype(BF16)


def coarse_forward(local, qc, arrived):
    tokens, width = qc.shape
    heads = width // HD
    whole = pl.BlockSpec((1, tokens, HD), lambda h: (0, 0, 0))
    return call(
        coarse_forward_kernel,
        6,
        grid=(heads,),
        in_specs=[whole] * 4
        + [spec(256, tokens // 256 - 1)]
        + [both(n) for n in ARRIVED],
        out_specs=[spec(tokens), lead(tokens, HD), both(KEYS)],
        out_shape=[
            jax.ShapeDtypeStruct((tokens, heads * HD), BF16),
            jax.ShapeDtypeStruct((heads, tokens, HD), F32),
            jax.ShapeDtypeStruct((KEYS, 2 * heads * HD), BF16),
        ],
        scratch_shapes=[pltpu.VMEM((B, HD), F32)] + [pltpu.VMEM((tokens, HD), F32)] * 2,
        name="coarse_forward",
    )(*local, qc, *arrived)


def with_dot(g, dot):
    lane = lax.broadcasted_iota(jnp.int32, dot.shape, 1)
    high = (-dot).astype(BF16)
    low = (-dot - high.astype(F32)).astype(BF16)
    zero = jnp.zeros(dot.shape, BF16)
    parts = jnp.where(lane == 0, high, jnp.where(lane == 1, low, zero))
    return jnp.concatenate([g.astype(BF16), parts], axis=1)


def backward_block(q, k, v, g, mask=None):
    expos = jnp.exp2(nt(k, q) * EXP_SCALE)
    if mask is not None:
        expos = jnp.where(mask, expos, 0.0)
    slopes = (expos * nt(with_ones(v), g)).astype(BF16)
    dq = tn(slopes, k)
    dk = nn(slopes, q)
    dv = nn(expos.astype(BF16), g[:, :HD])
    return dq, dk, dv


def coarse_backward_kernel(
    ga_ref, att_ref, rtot_ref, q_ref, side_ref, g0_ref, gc_ref, dq_ref, *refs
):
    sent, (g_scr, d_scr, small) = refs[:5], refs[5:]
    tokens = ga_ref.shape[0]
    step = 256
    for i in range(tokens // step):
        rows = slice(i * step, (i + 1) * step)
        ga = ga_ref[rows, :].astype(F32)
        rtot = rtot_ref[0, rows, :]
        g = ga * rtot
        dot = jnp.sum(ga * att_ref[rows, :].astype(F32), axis=1, keepdims=True) * rtot
        g_scr[rows, :] = g
        d_scr[rows, :] = dot
        g0_ref[0, rows, :] = with_dot(g, dot)
    for level in range(1, 9):
        n = tokens >> level
        here = offset(level, tokens)
        chunk = min(n, 256)
        for i in range(n // chunk):
            even, odd = pl.ds(2 * i * chunk, chunk, stride=2), pl.ds(2 * i * chunk + 1, chunk, stride=2)
            g = g_scr[even, :] + g_scr[odd, :]
            dot = d_scr[even, :] + d_scr[odd, :]
            g_scr[i * chunk:(i + 1) * chunk, :] = g
            d_scr[i * chunk:(i + 1) * chunk, :] = dot
            if n < 16:
                pad = jnp.zeros((16 - n, HD), F32)
                g, dot = jnp.concatenate([g, pad], axis=0), jnp.concatenate([dot, pad], axis=0)
            gc_ref[0, here + i * chunk:here + i * chunk + g.shape[0], :] = with_dot(g, dot)
    rows = q_ref.shape[0]
    level = level_of_row(lax.broadcasted_iota(jnp.int32, (KEYS, rows), 1))
    other = lax.broadcasted_iota(jnp.int32, (KEYS, rows), 0) // B
    g = gc_ref[0, tokens - rows:tokens, :]
    dq, dk, dv = backward_block(q_ref[...], side_ref[:, :HD], side_ref[:, HD:], g, level == other)
    dq_ref[0] = spread_levels(dq, small, 1.0)
    for lane, d in ((0, (dk * SCALE).astype(BF16)), (HD, dv.astype(BF16))):
        for i, ref in enumerate(sent):
            ref[:, lane:lane + HD] = d[i * B:(i + 1) * B, :]


def coarse_backward(ga, att, rtot, qc, side):
    heads, tokens, _ = rtot.shape
    wide = jax.ShapeDtypeStruct((heads, tokens, 2 * HD), BF16)
    return call(
        coarse_backward_kernel,
        6,
        grid=(heads,),
        in_specs=[spec(tokens)] * 2 + [lead(tokens, HD), spec(256, tokens // 256 - 1), both(KEYS)],
        out_specs=[lead(tokens, 2 * HD)] * 2 + [lead(B, HD)] + [both(B)] * 5,
        out_shape=[wide, wide, jax.ShapeDtypeStruct((heads, B, HD), F32)]
        + [jax.ShapeDtypeStruct((B, 2 * heads * HD), BF16)] * 5,
        scratch_shapes=[pltpu.VMEM((tokens, HD), F32)] * 2 + [pltpu.VMEM((B, HD), F32)],
        name="coarse_backward",
    )(ga, att, rtot, qc, side)


SCRATCH = 3 * (LOCAL - 1) + 1


def local_backward_kernel(
    q_ref, k_ref, v_ref, qc_ref, kc_ref, vc_ref, g0_ref, gc_ref, dq4_ref, *refs
):
    (dq_ref, dk_ref, dv_ref), scr = refs[-SCRATCH - 3:-SCRATCH], refs[-SCRATCH:]
    tokens = q_ref.shape[0]
    for level in range(LOCAL - 1, 0, -1):
        off = offset(level, tokens)
        sq, sk, sv = scr[3 * level - 3:3 * level]
        if level == LOCAL - 1:
            repeat2(dq4_ref[0], scr[3 * level])
        uq = scr[3 * level]
        uk, uv = scr[3 * level + 1:3 * level + 3] if level < LOCAL - 1 else (None, None)
        for i in range((tokens >> level) // 256):
            at = off + i * 256
            lo, hi = (at, i * 256), (at + B, i * 256 + B)
            for (ma, mr), (oa, orow) in ((lo, hi), (hi, lo)):
                mine, other = slice(ma, ma + B), slice(oa, oa + B)
                dq, dk, dv = backward_block(qc_ref[mine, :], kc_ref[other, :], vc_ref[other, :], gc_ref[0, mine, :])
                dq = dq + uq[mr:mr + B, :]
                if uk is not None:
                    dk = dk + uk[orow:orow + B, :]
                    dv = dv + uv[orow:orow + B, :]
                repeat2(dq, sq, 2 * mr)
                repeat2(dk, sk, 2 * orow)
                repeat2(dv, sv, 2 * orow)
    for i in range(tokens // 256):
        rows = slice(i * 256, (i + 1) * 256)
        dq, dk, dv = backward_block(q_ref[rows, :], k_ref[rows, :], v_ref[rows, :], g0_ref[0, rows, :])
        dq_ref[rows, :] = ((dq + scr[0][rows, :]) * SCALE).astype(BF16)
        dk_ref[rows, :] = ((dk + scr[1][rows, :]) * SCALE).astype(BF16)
        dv_ref[rows, :] = (dv + scr[2][rows, :]).astype(BF16)


def local_backward(head, inputs, before=()):
    tokens, width = inputs[0].shape
    scratch = []
    for level in range(1, LOCAL):
        scratch += [pltpu.VMEM((tokens >> (level - 1), HD), F32)] * 3
    scratch += [pltpu.VMEM((tokens >> (LOCAL - 1), HD), F32)]
    columns = pl.BlockSpec((tokens, HD), lambda i: (0, head))
    wide = pl.BlockSpec((1, tokens, 2 * HD), lambda i: (head, 0, 0))
    small = pl.BlockSpec((1, B, HD), lambda i: (head, 0, 0))
    return call(
        local_backward_kernel,
        8,
        grid=(1,),
        in_specs=[columns] * 6 + [wide] * 2 + [small] + [pl.BlockSpec(memory_space=pl.ANY)] * len(before),
        out_specs=[columns] * 3,
        out_shape=[jax.ShapeDtypeStruct((tokens, width), BF16)] * 3,
        scratch_shapes=scratch,
        input_output_aliases={9 + i: i for i in range(len(before))},
        name="local_backward",
    )(*inputs, *before)


def finish_kernel(dk_ref, dv_ref, own, r1, r2, r3, gk_ref, gv_ref, small, big):
    for part, lane, out in ((dk_ref, 0, gk_ref), (dv_ref, HD, gv_ref)):
        rows = lambda ref, lo, hi: ref[lo:hi, lane:lane + HD].astype(F32)
        x4 = rows(r1, 0, 128)
        x5 = rows(r2, 0, 64) + rows(r3, 0, 64)
        rest = rows(own, 0, 64) + rows(r1, 128, 192) + rows(r2, 64, 128) + rows(r3, 64, 128)
        repeat16(spread_levels(jnp.concatenate([x4, x5, rest], axis=0), small, 1.0), big)
        out[...] = (part[...].astype(F32) + big[...]).astype(BF16)


def finish(dk, dv, returned):
    tokens, width = dk.shape
    shape = jax.ShapeDtypeStruct((tokens, width), BF16)
    return call(
        finish_kernel,
        4,
        grid=(width // HD,),
        in_specs=[spec(tokens)] * 2 + [both(n) for n in (64, 192, 128, 128)],
        out_specs=[spec(tokens)] * 2,
        out_shape=[shape] * 2,
        scratch_shapes=[pltpu.VMEM((B, HD), F32), pltpu.VMEM((tokens, HD), F32)],
        name="finish",
    )(dk, dv, *returned)


def mix_kernel(att_ref, w_ref, out_ref, held, sem):
    shards, _, width = att_ref.shape
    chunk = 512
    copies = []
    for c in range(out_ref.shape[1] // chunk):
        columns = pl.ds(c * chunk, chunk)
        copies.append(pltpu.make_async_copy(w_ref.at[:, columns], held.at[:, columns], sem.at[c]))
        copies[-1].start()
    att = jnp.concatenate([att_ref[j] for j in range(shards)], axis=1)
    for c, copy in enumerate(copies):
        columns = slice(c * chunk, (c + 1) * chunk)
        copy.wait()
        out_ref[:, columns] = nn(att, held[:, columns]).astype(BF16)


def mix(att, w):
    shards, rows, width = att.shape
    whole = pl.BlockSpec(memory_space=pltpu.VMEM)
    return call(
        mix_kernel,
        6,
        in_specs=[whole, pl.BlockSpec(memory_space=pl.ANY)],
        out_specs=whole,
        out_shape=jax.ShapeDtypeStruct((rows, w.shape[1]), BF16),
        scratch_shapes=[pltpu.VMEM(w.shape, BF16), pltpu.SemaphoreType.DMA((w.shape[1] // 512,))],
        name="mix",
    )(att, w)


def swap(x, axis, distance):
    return lax.ppermute(x, axis, [(i, i ^ distance) for i in range(lax.axis_size(axis))])


def after(x, *others):
    return lax.optimization_barrier((x,) + others)[0]


def cat(parts):
    return jnp.concatenate(parts, axis=0)


def levels_of(x):
    n = x.shape[0]
    return x[n - 64:n - 32], x[n - 32:n - 16], x[n - 16:n - 8]


def add(*parts):
    return sum(x.astype(F32) for x in parts).astype(BF16)


def quarters(x, place):
    n = x.shape[0] // 4
    return [lax.dynamic_slice_in_dim(x, (place ^ j) * n, n, 0) for j in range(4)]


def join_quarters(parts, place):
    n = parts[0].shape[0]
    whole = jnp.zeros((4 * n,) + parts[0].shape[1:], parts[0].dtype)
    for j, y in enumerate(parts):
        whole = lax.dynamic_update_slice_in_dim(whole, y, (place ^ j) * n, 0)
    return whole


def body(queries, keys, values, w_out, grad_out):
    tokens, width = queries.shape
    shards = lax.axis_size("head")
    assert shards == 8 and lax.axis_size("seq") == 32
    y, z = lax.axis_index("seq") >> 3, lax.axis_index("seq") & 3
    cotangent = lax.all_gather(grad_out, "head", axis=0, tiled=True)
    w_full = lax.all_gather(w_out, "head", axis=0, tiled=True)

    qc, kc, vc, m1, m2 = coarsen(queries, keys, values)
    near = [swap(m1, "seq", 1), swap(m2, "seq", 2), swap(m2, "seq", 3)]
    inputs = (queries, keys, values, qc, kc)
    local = tuple(local_forward(0, *inputs, vc))
    near = after(tuple(near), local[0])
    six, seven, eight = (cat(parts) for parts in zip(*[levels_of(x) for x in (m1, *near)]))
    group = cat([seven, eight])
    far = [swap(cat([six, eight]), "seq", 4), swap(group, "seq", 8), swap(group, "seq", 12)]
    local += tuple(local_forward(1, *inputs, after(vc, six)))
    far = after(tuple(far), local[2])
    last = swap(cat([eight] + [x[x.shape[0] - 32:] for x in far]), "seq", 16)
    attended, rtot, side = coarse_forward(local, qc, (*near, *far, last))

    mine = lax.all_to_all(attended.reshape(shards, tokens // shards, width), "head", 0, 0)
    grad_weight = tn(attended, cotangent).astype(BF16)
    ga = nt(cotangent, after(w_out, grad_weight)).astype(BF16)
    own, *rest = quarters(grad_weight, y)
    rest = [swap(x, "seq", 8 * (j + 1)) for j, x in enumerate(rest)]
    g0, gc, dq4, e4, e5, e6, e7, e8 = coarse_backward(ga, attended, rtot, qc, side)
    rest = after(tuple(rest), dq4)
    partial = add(own, *rest)
    mine = after(mine, dq4)

    x8 = swap(e8, "seq", 16)
    own, *rest = quarters(partial, z)
    rest = [swap(x, "seq", j + 1) for j, x in enumerate(rest)]
    inputs = (queries, keys, values, qc, kc, vc, g0, gc)
    done = local_backward(0, inputs + (after(dq4, partial),))
    rest, x8 = after((rest, x8), done[0])
    partial = add(own, *rest)

    f4 = swap(cat([e6, x8[32:64]]), "seq", 4)
    f8 = swap(cat([e7[:64], x8[64:96]]), "seq", 8)
    f12 = swap(cat([e7[64:], x8[96:]]), "seq", 12)
    low = swap(partial, "seq", 4)
    grad_q, dk, dv = local_backward(1, inputs + (after(dq4, partial, x8),), done)
    low, f4, f8, f12 = after((low, f4, f8, f12), grad_q)
    partial = add(partial, low)

    x6, x7, x8 = f4[:B], add(f8[:64], f12[:64]), add(x8[:32], f4[B:], f8[64:], f12[64:])
    first = [e4, e5[:64], e5[64:]]
    pad = jnp.zeros((8, x8.shape[1]), BF16)
    tails = [cat([x6[32 * j:][:32], x7[16 * j:][:16], x8[8 * j:][:8], pad]) for j in range(4)]
    near = [swap(cat([x, tails[j + 1]]), "seq", j + 1) for j, x in enumerate(first)]
    rest = [swap(partial, "seq", j) for j in (1, 2, 3)]
    mixed = mix(after(mine, partial, tails[0]), w_full)
    rest, near = after((rest, near), mixed)
    summed = join_quarters([partial] + rest, z)

    parts = [summed] + [swap(summed, "seq", j << 3) for j in (1, 2, 3)]
    grad_k, grad_v = finish(after(dk, summed), dv, (tails[0], *near))
    parts = after(parts, grad_k)
    return mixed, grad_q, grad_k, grad_v, join_quarters(parts, y)


def solution(mesh):
    return jax.shard_map(
        body,
        mesh=mesh,
        in_specs=(
            P("seq", "head"),
            P("seq", "head"),
            P("seq", "head"),
            P("head", None),
            P(("seq", "head"), None),
        ),
        out_specs=(
            P(("seq", "head"), None),
            P("seq", "head"),
            P("seq", "head"),
            P("seq", "head"),
            P("head", None),
        ),
        check_vma=False,
    )
```

```python
import functools
import jax
import jax.numpy as jnp
from jax import lax
from jax.experimental import pallas as pl
from jax.experimental.pallas import tpu as pltpu
from jax.sharding import PartitionSpec as P

HD = 128
B = 128
LOCAL = 4
F32 = jnp.float32
BF16 = jnp.bfloat16
EXP_SCALE = 1.4426950408889634 * HD ** (-0.5)
SCALE = HD ** (-0.5)
VMEM = 56 * 1024 * 1024
COST = 0.05e6


def nn(a, b):
    return lax.dot_general(a, b, (((1,), (0,)), ((), ())), preferred_element_type=F32)


def nt(a, b):
    return lax.dot_general(a, b, (((1,), (1,)), ((), ())), preferred_element_type=F32)


def tn(a, b):
    return lax.dot_general(a, b, (((0,), (0,)), ((), ())), preferred_element_type=F32)


def call(kernel, micros, **kwargs):
    cost = pl.CostEstimate(flops=0, bytes_accessed=int(micros * COST), transcendentals=0)
    return pl.pallas_call(
        kernel,
        cost_estimate=cost,
        compiler_params=pltpu.CompilerParams(vmem_limit_bytes=VMEM),
        **kwargs,
    )


def offset(level, tokens):
    return tokens - (tokens >> (level - 1))


def spec(rows, block=0):
    return pl.BlockSpec((rows, HD), lambda h: (block, h))


def lead(rows, width):
    return pl.BlockSpec((1, rows, width), lambda h: (h, 0, 0))


def both(rows):
    return pl.BlockSpec((rows, 2 * HD), lambda h: (0, h))


def with_ones(v):
    return jnp.concatenate([v, jnp.ones(v.shape, BF16)], axis=1)


def repeat2(x, scratch, base=0):
    n = x.shape[0]
    scratch[pl.ds(base, n, stride=2), :] = x
    scratch[pl.ds(base + 1, n, stride=2), :] = x


def coarsen_kernel(q_ref, k_ref, v_ref, qc_ref, kc_ref, vc_ref, m1_ref, m2_ref):
    tokens = q_ref.shape[0]
    r = lax.broadcasted_iota(jnp.int32, (B, 2 * B), 0)
    c = lax.broadcasted_iota(jnp.int32, (B, 2 * B), 1)
    mean = jnp.where(c // 2 == r, 0.5, 0.0).astype(BF16)
    half = mean[:64, :128]
    for src, dst in ((q_ref, qc_ref), (k_ref, kc_ref), (v_ref, vc_ref)):
        for i in range(tokens // 256):
            dst[i * B:(i + 1) * B, :] = nn(mean, src[i * 256:(i + 1) * 256, :]).astype(BF16)
    for level in range(2, LOCAL + 1):
        before, here = offset(level - 1, tokens), offset(level, tokens)
        for dst in (qc_ref, kc_ref, vc_ref):
            for i in range((tokens >> level) // B):
                rows = dst[before + i * 256:before + (i + 1) * 256, :]
                dst[here + i * B:here + (i + 1) * B, :] = nn(mean, rows).astype(BF16)
    tail = offset(LOCAL + 1, tokens)
    for dst in (qc_ref, kc_ref, vc_ref):
        x5 = nn(half, dst[tail - B:tail, :]).astype(BF16)
        x6 = nn(half[:32, :64], x5).astype(BF16)
        x7 = nn(half[:16, :32], x6).astype(BF16)
        x8 = nn(half[:16, :16], x7).astype(BF16)
        dst[tail:tail + 64, :] = x5
        dst[tail + 64:tail + 96, :] = x6
        dst[tail + 96:tail + 112, :] = x7
        dst[tail + 112:tail + 128, :] = x8
    tail = tokens - 64
    for lane, src in ((0, kc_ref), (HD, vc_ref)):
        columns = slice(lane, lane + HD)
        m1_ref[:B, columns] = src[tokens - 256:tokens - 128, :]
        m2_ref[:64, columns] = src[tokens - 128:tail, :]
        m1_ref[B:, columns] = src[tail:, :]
        m2_ref[64:, columns] = src[tail:, :]


def coarsen(q, k, v):
    shape = jax.ShapeDtypeStruct(q.shape, BF16)
    tokens, width = q.shape
    sizes = (192, 128)
    return call(
        coarsen_kernel,
        6,
        grid=(width // HD,),
        in_specs=[spec(tokens)] * 3,
        out_specs=[spec(tokens)] * 3 + [both(n) for n in sizes],
        out_shape=[shape] * 3 + [jax.ShapeDtypeStruct((n, 2 * width), BF16) for n in sizes],
        name="coarsen",
    )(q, k, v)


def forward_blocks(blocks):
    scores = [nt(q, k) for q, k, _ in blocks]
    expos = [jnp.exp2(x * EXP_SCALE).astype(BF16) for x in scores]
    return [nn(e, with_ones(v)) for e, (_, _, v) in zip(expos, blocks)]


def sibling_pairs(level, tokens):
    off = offset(level, tokens)
    for i in range(0, tokens >> level, 256):
        lo, hi = (off + i, i), (off + i + B, i + B)
        yield lo, hi
        yield hi, lo


def local_forward_kernel(q_ref, k_ref, v_ref, qc_ref, kc_ref, vc_ref, numer_ref, total_ref, *scr):
    tokens = q_ref.shape[0]
    for levels in ((3, 2), (1,)):
        pairs = [(level, *pair) for level in levels for pair in sibling_pairs(level, tokens)]
        blocks = []
        for _, (ma, _), (oa, _) in pairs:
            mine, other = slice(ma, ma + B), slice(oa, oa + B)
            blocks.append((qc_ref[mine, :], kc_ref[other, :], vc_ref[other, :]))
        for (level, (_, at), _), u in zip(pairs, forward_blocks(blocks)):
            n, t = u[:, :HD], u[:, HD:]
            if level < LOCAL - 1:
                n = n + 2.0 * scr[2 * level][at:at + B, :]
                t = t + 2.0 * scr[2 * level + 1][at:at + B, :]
            repeat2(n, scr[2 * level - 2], 2 * at)
            repeat2(t, scr[2 * level - 1], 2 * at)
    for i in range(0, tokens, 1024):
        rows = [slice(at, at + 256) for at in range(i, i + 1024, 256)]
        sums = forward_blocks([(q_ref[r, :], k_ref[r, :], v_ref[r, :]) for r in rows])
        for r, u in zip(rows, sums):
            numer_ref[0, r, :] = u[:, :HD] + 2.0 * scr[0][r, :]
            total_ref[0, r, :] = u[:, HD:] + 2.0 * scr[1][r, :]


def local_forward(head, q, k, v, qc, kc, vc):
    tokens, width = q.shape
    scratch = []
    for level in range(1, LOCAL):
        scratch += [pltpu.VMEM((tokens >> (level - 1), HD), F32)] * 2
    columns = pl.BlockSpec((tokens, HD), lambda i: (0, head))
    return call(
        local_forward_kernel,
        5,
        grid=(1,),
        in_specs=[columns] * 6,
        out_specs=[lead(tokens, HD)] * 2,
        out_shape=[jax.ShapeDtypeStruct((1, tokens, HD), F32)] * 2,
        scratch_shapes=scratch,
        name="local_forward",
    )(q, k, v, qc, kc, vc)


def level_of_row(row):
    steps = [(row >= edge).astype(jnp.int32) for edge in (128, 192, 224, 240, 248)]
    return sum(steps)


KEYS = 640
ARRIVED = (192, 128, 128, 160, 96, 96, 128)
USED = (128, 64, 64, 128, 64, 64, 128)


def spread_levels(packed, scratch, weight):
    bounds = (0, 128, 192, 224, 240, 248)
    x = packed[240:248, :]
    for i in range(3, -1, -1):
        lo, hi = bounds[i], bounds[i + 1]
        repeat2(x, scratch)
        x = packed[lo:hi, :] + weight * scratch[0:hi - lo, :]
    return x


def repeat16(x):
    high = x.astype(BF16)
    low = (x - high.astype(F32)).astype(BF16)
    r = lax.broadcasted_iota(jnp.int32, (256, 32), 0)
    c = lax.broadcasted_iota(jnp.int32, (256, 32), 1)
    copies = jnp.where((r >> 4) == (c & 15), 1.0, 0.0).astype(BF16)
    for i in range(x.shape[0] // 16):
        part = slice(i * 16, i * 16 + 16)
        yield slice(i * 256, i * 256 + 256), nn(copies, jnp.concatenate([high[part], low[part]], axis=0))


def coarse_forward_kernel(numer0, total0, numer1, total1, q_ref, *refs):
    arrived, (att_ref, rtot_ref, side_ref, small) = refs[:7], refs[7:]
    at = 0
    for ref, n in zip(arrived, USED):
        side_ref[at:at + n, :] = ref[:n, :]
        at += n
    rows = q_ref.shape[0]
    level = level_of_row(lax.broadcasted_iota(jnp.int32, (rows, KEYS), 0))
    other = lax.broadcasted_iota(jnp.int32, (rows, KEYS), 1) // B
    expos = jnp.where(level == other, jnp.exp2(nt(q_ref[...], side_ref[:, :HD]) * EXP_SCALE), 0.0)
    u = nn(expos.astype(BF16), with_ones(side_ref[:, HD:]))
    parts = [16.0 * spread_levels(u[:, half], small, 2.0) for half in (slice(0, HD), slice(HD, None))]
    coarse = jnp.concatenate(parts, axis=1)
    for head, numer_ref, total_ref in ((0, numer0, total0), (1, numer1, total1)):

        @pl.when(pl.program_id(0) == head)
        def _():
            for at, x in repeat16(coarse):
                rtot = 1.0 / (total_ref[0, at, :] + x[:, HD:])
                rtot_ref[0, at, :] = rtot
                att_ref[at, :] = ((numer_ref[0, at, :] + x[:, :HD]) * rtot).astype(BF16)


def coarse_forward(local, qc, arrived):
    tokens, width = qc.shape
    heads = width // HD
    whole = pl.BlockSpec((1, tokens, HD), lambda h: (0, 0, 0))
    return call(
        coarse_forward_kernel,
        6,
        grid=(heads,),
        in_specs=[whole] * 4
        + [spec(256, tokens // 256 - 1)]
        + [both(n) for n in ARRIVED],
        out_specs=[spec(tokens), lead(tokens, HD), both(KEYS)],
        out_shape=[
            jax.ShapeDtypeStruct((tokens, heads * HD), BF16),
            jax.ShapeDtypeStruct((heads, tokens, HD), F32),
            jax.ShapeDtypeStruct((KEYS, 2 * heads * HD), BF16),
        ],
        scratch_shapes=[pltpu.VMEM((B, HD), F32)],
        name="coarse_forward",
    )(*local, qc, *arrived)


def with_dot(g, dot):
    lane = lax.broadcasted_iota(jnp.int32, dot.shape, 1)
    high = (-dot).astype(BF16)
    low = (-dot - high.astype(F32)).astype(BF16)
    zero = jnp.zeros(dot.shape, BF16)
    parts = jnp.where(lane == 0, high, jnp.where(lane == 1, low, zero))
    return jnp.concatenate([g.astype(BF16), parts], axis=1)


def backward_blocks(blocks, mask=None):
    scores = [nt(k, q) for q, k, _, _ in blocks]
    probes = [nt(with_ones(v), g) for _, _, v, g in blocks]
    expos = [jnp.exp2(x * EXP_SCALE) for x in scores]
    if mask is not None:
        expos = [jnp.where(mask, e, 0.0) for e in expos]
    slopes = [(e * p).astype(BF16) for e, p in zip(expos, probes)]
    dv = [nn(e.astype(BF16), g[:, :HD]) for e, (_, _, _, g) in zip(expos, blocks)]
    dk = [nn(s, q) for s, (q, _, _, _) in zip(slopes, blocks)]
    dq = [tn(s, k) for s, (_, k, _, _) in zip(slopes, blocks)]
    return list(zip(dq, dk, dv))


def coarse_backward_kernel(
    ga_ref, att_ref, rtot_ref, q_ref, side_ref, g0_ref, gc_ref, dq_ref, *refs
):
    sent, (g_scr, d_scr, small) = refs[:5], refs[5:]
    tokens = ga_ref.shape[0]
    step = 256
    for i in range(tokens // step):
        rows = slice(i * step, (i + 1) * step)
        ga = ga_ref[rows, :].astype(F32)
        rtot = rtot_ref[0, rows, :]
        g = ga * rtot
        dot = jnp.sum(ga * att_ref[rows, :].astype(F32), axis=1, keepdims=True) * rtot
        g_scr[rows, :] = g
        d_scr[rows, :] = dot
        g0_ref[0, rows, :] = with_dot(g, dot)
    for level in range(1, 9):
        n = tokens >> level
        here = offset(level, tokens)
        chunk = min(n, 256)
        for i in range(n // chunk):
            even, odd = pl.ds(2 * i * chunk, chunk, stride=2), pl.ds(2 * i * chunk + 1, chunk, stride=2)
            g = g_scr[even, :] + g_scr[odd, :]
            dot = d_scr[even, :] + d_scr[odd, :]
            g_scr[i * chunk:(i + 1) * chunk, :] = g
            d_scr[i * chunk:(i + 1) * chunk, :] = dot
            if n < 16:
                pad = jnp.zeros((16 - n, HD), F32)
                g, dot = jnp.concatenate([g, pad], axis=0), jnp.concatenate([dot, pad], axis=0)
            gc_ref[0, here + i * chunk:here + i * chunk + g.shape[0], :] = with_dot(g, dot)
    rows = q_ref.shape[0]
    level = level_of_row(lax.broadcasted_iota(jnp.int32, (KEYS, rows), 1))
    other = lax.broadcasted_iota(jnp.int32, (KEYS, rows), 0) // B
    g = gc_ref[0, tokens - rows:tokens, :]
    block = (q_ref[...], side_ref[:, :HD], side_ref[:, HD:], g)
    (dq, dk, dv), = backward_blocks([block], level == other)
    dq_ref[0] = spread_levels(dq, small, 1.0)
    for lane, d in ((0, (dk * SCALE).astype(BF16)), (HD, dv.astype(BF16))):
        for i, ref in enumerate(sent):
            ref[:, lane:lane + HD] = d[i * B:(i + 1) * B, :]


def coarse_backward(ga, att, rtot, qc, side):
    heads, tokens, _ = rtot.shape
    wide = jax.ShapeDtypeStruct((heads, tokens, 2 * HD), BF16)
    return call(
        coarse_backward_kernel,
        6,
        grid=(heads,),
        in_specs=[spec(tokens)] * 2 + [lead(tokens, HD), spec(256, tokens // 256 - 1), both(KEYS)],
        out_specs=[lead(tokens, 2 * HD)] * 2 + [lead(B, HD)] + [both(B)] * 5,
        out_shape=[wide, wide, jax.ShapeDtypeStruct((heads, B, HD), F32)]
        + [jax.ShapeDtypeStruct((B, 2 * heads * HD), BF16)] * 5,
        scratch_shapes=[pltpu.VMEM((tokens, HD), F32)] * 2 + [pltpu.VMEM((B, HD), F32)],
        name="coarse_backward",
    )(ga, att, rtot, qc, side)


SCRATCH = 3 * (LOCAL - 1) + 1


def local_backward_kernel(
    q_ref, k_ref, v_ref, qc_ref, kc_ref, vc_ref, g0_ref, gc_ref, dq4_ref, *refs
):
    (dq_ref, dk_ref, dv_ref), scr = refs[-SCRATCH - 3:-SCRATCH], refs[-SCRATCH:]
    tokens = q_ref.shape[0]
    repeat2(dq4_ref[0], scr[3 * (LOCAL - 1)])
    for levels in ((3, 2), (1,)):
        pairs = [(level, *pair) for level in levels for pair in sibling_pairs(level, tokens)]
        blocks = []
        for _, (ma, _), (oa, _) in pairs:
            mine, other = slice(ma, ma + B), slice(oa, oa + B)
            blocks.append((qc_ref[mine, :], kc_ref[other, :], vc_ref[other, :], gc_ref[0, mine, :]))
        for (level, (_, mr), (_, orow)), (dq, dk, dv) in zip(pairs, backward_blocks(blocks)):
            dq = dq + scr[3 * level][mr:mr + B, :]
            if level < LOCAL - 1:
                dk = dk + scr[3 * level + 1][orow:orow + B, :]
                dv = dv + scr[3 * level + 2][orow:orow + B, :]
            repeat2(dq, scr[3 * level - 3], 2 * mr)
            repeat2(dk, scr[3 * level - 2], 2 * orow)
            repeat2(dv, scr[3 * level - 1], 2 * orow)
    for i in range(0, tokens, 512):
        rows = [slice(at, at + 256) for at in range(i, i + 512, 256)]
        blocks = [(q_ref[r, :], k_ref[r, :], v_ref[r, :], g0_ref[0, r, :]) for r in rows]
        for r, (dq, dk, dv) in zip(rows, backward_blocks(blocks)):
            dq_ref[r, :] = ((dq + scr[0][r, :]) * SCALE).astype(BF16)
            dk_ref[r, :] = ((dk + scr[1][r, :]) * SCALE).astype(BF16)
            dv_ref[r, :] = (dv + scr[2][r, :]).astype(BF16)


def local_backward(head, inputs, before=()):
    tokens, width = inputs[0].shape
    scratch = []
    for level in range(1, LOCAL):
        scratch += [pltpu.VMEM((tokens >> (level - 1), HD), F32)] * 3
    scratch += [pltpu.VMEM((tokens >> (LOCAL - 1), HD), F32)]
    columns = pl.BlockSpec((tokens, HD), lambda i: (0, head))
    wide = pl.BlockSpec((1, tokens, 2 * HD), lambda i: (head, 0, 0))
    small = pl.BlockSpec((1, B, HD), lambda i: (head, 0, 0))
    return call(
        local_backward_kernel,
        8,
        grid=(1,),
        in_specs=[columns] * 6 + [wide] * 2 + [small] + [pl.BlockSpec(memory_space=pl.ANY)] * len(before),
        out_specs=[columns] * 3,
        out_shape=[jax.ShapeDtypeStruct((tokens, width), BF16)] * 3,
        scratch_shapes=scratch,
        input_output_aliases={9 + i: i for i in range(len(before))},
        name="local_backward",
    )(*inputs, *before)


def finish_kernel(dk_ref, dv_ref, own, r1, r2, r3, gk_ref, gv_ref, small):
    rows = lambda ref, lo, hi: ref[lo:hi, :].astype(F32)
    x4 = rows(r1, 0, 128)
    x5 = rows(r2, 0, 64) + rows(r3, 0, 64)
    rest = rows(own, 0, 64) + rows(r1, 128, 192) + rows(r2, 64, 128) + rows(r3, 64, 128)
    packed = jnp.concatenate([x4, x5, rest], axis=0)
    parts = [spread_levels(packed[:, half], small, 1.0) for half in (slice(0, HD), slice(HD, None))]
    for at, x in repeat16(jnp.concatenate(parts, axis=1)):
        gk_ref[at, :] = (dk_ref[at, :].astype(F32) + x[:, :HD]).astype(BF16)
        gv_ref[at, :] = (dv_ref[at, :].astype(F32) + x[:, HD:]).astype(BF16)


def finish(dk, dv, returned):
    tokens, width = dk.shape
    shape = jax.ShapeDtypeStruct((tokens, width), BF16)
    return call(
        finish_kernel,
        4,
        grid=(width // HD,),
        in_specs=[spec(tokens)] * 2 + [both(n) for n in (64, 256, 128, 128)],
        out_specs=[spec(tokens)] * 2,
        out_shape=[shape] * 2,
        scratch_shapes=[pltpu.VMEM((B, HD), F32)],
        name="finish",
    )(dk, dv, *returned)


def mix_kernel(att_ref, w_ref, out_ref, held, sem):
    shards, _, width = att_ref.shape
    chunk = 512
    copies = []
    for c in range(out_ref.shape[1] // chunk):
        columns = pl.ds(c * chunk, chunk)
        copies.append(pltpu.make_async_copy(w_ref.at[:, columns], held.at[:, columns], sem.at[c]))
        copies[-1].start()
    att = jnp.concatenate([att_ref[j] for j in range(shards)], axis=1)
    for c, copy in enumerate(copies):
        columns = slice(c * chunk, (c + 1) * chunk)
        copy.wait()
        out_ref[:, columns] = nn(att, held[:, columns]).astype(BF16)


def mix(att, w):
    shards, rows, width = att.shape
    whole = pl.BlockSpec(memory_space=pltpu.VMEM)
    return call(
        mix_kernel,
        6,
        in_specs=[whole, pl.BlockSpec(memory_space=pl.ANY)],
        out_specs=whole,
        out_shape=jax.ShapeDtypeStruct((rows, w.shape[1]), BF16),
        scratch_shapes=[pltpu.VMEM(w.shape, BF16), pltpu.SemaphoreType.DMA((w.shape[1] // 512,))],
        name="mix",
    )(att, w)


def swap(x, axis, distance):
    return lax.ppermute(x, axis, [(i, i ^ distance) for i in range(lax.axis_size(axis))])


def swap_z(x, distance):
    place = lambda i: (i & 24) | ((((i - 2) & 7) ^ distance) + 2) & 7
    return lax.ppermute(x, "seq", [(i, place(i)) for i in range(lax.axis_size("seq"))])


def shift_y(x, distance):
    n = lax.axis_size("seq")
    return lax.ppermute(x, "seq", [(i, (i + 8 * distance) % n) for i in range(n)])


def after(x, *others):
    return lax.optimization_barrier((x,) + others)[0]


def cat(parts):
    return jnp.concatenate(parts, axis=0)


def levels_of(x):
    n = x.shape[0]
    return x[n - 64:n - 32], x[n - 32:n - 16], x[n - 16:n - 8]


def add(*parts):
    return sum(x.astype(F32) for x in parts).astype(BF16)


def quarters(x, place, axis):
    n = x.shape[axis] // 4
    return [lax.dynamic_slice_in_dim(x, (place ^ j) * n, n, axis) for j in range(4)]


def join_quarters(parts, places, axis):
    n = parts[0].shape[axis]
    whole = jnp.concatenate([jnp.zeros(p.shape, p.dtype) for p in parts], axis)
    for place, part in zip(places, parts):
        whole = lax.dynamic_update_slice_in_dim(whole, part, place * n, axis)
    return whole


def body(queries, keys, values, w_out, grad_out):
    tokens, width = queries.shape
    shards = lax.axis_size("head")
    assert shards == 8 and lax.axis_size("seq") == 32
    y, z = lax.axis_index("seq") >> 3, (lax.axis_index("seq") - 2) & 7
    z = (z & 3) ^ (3 * (z >> 2))
    cotangent = lax.all_gather(grad_out, "head", axis=0, tiled=True)
    w_full = lax.all_gather(w_out, "head", axis=0, tiled=True)

    qc, kc, vc, m1, m2 = coarsen(queries, keys, values)
    near = [swap(m1, "seq", 1), swap(m2, "seq", 2), swap(m2, "seq", 3)]
    inputs = (queries, keys, values, qc, kc)
    local = tuple(local_forward(0, *inputs, vc))
    near = after(tuple(near), local[0])
    six, seven, eight = (cat(parts) for parts in zip(*[levels_of(x) for x in (m1, *near)]))
    group = cat([seven, eight])
    far = [swap(cat([six, eight]), "seq", 7), swap(group, "seq", 8), swap(group, "seq", 15)]
    local += tuple(local_forward(1, *inputs, after(vc, six)))
    far = after(tuple(far), local[2])
    last = swap(cat([eight] + [x[x.shape[0] - 32:] for x in far]), "seq", 24)
    attended, rtot, side = coarse_forward(local, qc, (*near, *far, last))

    mine = lax.all_to_all(attended.reshape(shards, tokens // shards, width), "head", 0, 0)
    grad_weight = tn(attended, cotangent).astype(BF16)
    ga = nt(cotangent, after(w_out, grad_weight)).astype(BF16)
    own, *rest = quarters(grad_weight, y, 1)
    rest = [swap(x, "seq", 8 * (j + 1)) for j, x in enumerate(rest)]
    g0, gc, dq4, e4, e5, e6, e7, e8 = coarse_backward(ga, attended, rtot, qc, side)
    rest = after(tuple(rest), dq4)
    partial = add(own, *rest)
    mine = after(mine, dq4)

    x8 = swap(e8, "seq", 24)
    own, *rest = quarters(partial, z, 0)
    rest = [swap_z(x, j + 1) for j, x in enumerate(rest)]
    inputs = (queries, keys, values, qc, kc, vc, g0, gc)
    done = local_backward(0, inputs + (after(dq4, partial),))
    rest, x8 = after((rest, x8), done[0])
    partial = add(own, *rest)

    f7 = swap(cat([e6, x8[32:64]]), "seq", 7)
    f8 = swap(cat([e7[:64], x8[64:96]]), "seq", 8)
    f15 = swap(cat([e7[64:], x8[96:]]), "seq", 15)
    low = swap_z(partial, 7)
    grad_q, dk, dv = local_backward(1, inputs + (after(dq4, partial, x8),), done)
    low, f7, f8, f15 = after((low, f7, f8, f15), grad_q)
    partial = add(partial, low)

    x6, x7, x8 = f7[:B], add(f8[:64], f15[:64]), add(x8[:32], f7[B:], f8[64:], f15[64:])
    first = [e4, e5[:64], e5[64:]]
    pad = jnp.zeros((8, x8.shape[1]), BF16)
    tails = [cat([x6[32 * j:][:32], x7[16 * j:][:16], x8[8 * j:][:8], pad]) for j in range(4)]
    messages = [[x, tails[j + 1]] for j, x in enumerate(first)]
    messages[0].append(partial)
    near = [swap(cat(x), "seq", j + 1) for j, x in enumerate(messages)]
    rest = [swap_z(partial, j) for j in (2, 3)]
    mixed = mix(after(mine, partial, tails[0]), w_full)
    near, rest = after((near, rest), mixed)
    summed = join_quarters([partial, near[0][192:]] + rest, [z ^ j for j in range(4)], 0)

    up, down = shift_y(summed, 1), shift_y(summed, -1)
    grad_k, grad_v = finish(after(dk, summed), dv, (tails[0], *near))
    up, down = after((up, down), grad_k)
    far = cat([shift_y(up[:B], 1), shift_y(down[B:], -1)])
    places = [y, (y + 3) & 3, (y + 1) & 3, (y + 2) & 3]
    return mixed, grad_q, grad_k, grad_v, join_quarters([summed, up, down, far], places, 1)


def solution(mesh):
    return jax.shard_map(
        body,
        mesh=mesh,
        in_specs=(
            P("seq", "head"),
            P("seq", "head"),
            P("seq", "head"),
            P("head", None),
            P(("seq", "head"), None),
        ),
        out_specs=(
            P(("seq", "head"), None),
            P("seq", "head"),
            P("seq", "head"),
            P("seq", "head"),
            P("head", None),
        ),
        check_vma=False,
    )
```

```python
import functools
import jax
import jax.numpy as jnp
from jax import lax
from jax.experimental import pallas as pl
from jax.experimental.pallas import tpu as pltpu
from jax.sharding import PartitionSpec as P

HD = 128
B = 128
LOCAL = 4
F32 = jnp.float32
BF16 = jnp.bfloat16
EXP_SCALE = 1.4426950408889634 * HD ** (-0.5)
SCALE = HD ** (-0.5)
VMEM = 56 * 1024 * 1024
COST = 0.05e6


def nn(a, b):
    return lax.dot_general(a, b, (((1,), (0,)), ((), ())), preferred_element_type=F32)


def nt(a, b):
    return lax.dot_general(a, b, (((1,), (1,)), ((), ())), preferred_element_type=F32)


def tn(a, b):
    return lax.dot_general(a, b, (((0,), (0,)), ((), ())), preferred_element_type=F32)


def call(kernel, micros, **kwargs):
    cost = pl.CostEstimate(flops=0, bytes_accessed=int(micros * COST), transcendentals=0)
    return pl.pallas_call(
        kernel,
        cost_estimate=cost,
        compiler_params=pltpu.CompilerParams(vmem_limit_bytes=VMEM),
        **kwargs,
    )


def offset(level, tokens):
    return tokens - (tokens >> (level - 1))


def spec(rows, block=0):
    return pl.BlockSpec((rows, HD), lambda h: (block, h))


def lead(rows, width):
    return pl.BlockSpec((1, rows, width), lambda h: (h, 0, 0))


def both(rows):
    return pl.BlockSpec((rows, 2 * HD), lambda h: (0, h))


def with_ones(v):
    return jnp.concatenate([v, jnp.ones(v.shape, BF16)], axis=1)


def repeat2(x, scratch, base=0):
    n = x.shape[0]
    scratch[pl.ds(base, n, stride=2), :] = x
    scratch[pl.ds(base + 1, n, stride=2), :] = x


def coarsen_kernel(q_ref, k_ref, v_ref, qc_ref, kc_ref, vc_ref, m1_ref, m2_ref):
    tokens = q_ref.shape[0]
    r = lax.broadcasted_iota(jnp.int32, (B, 2 * B), 0)
    c = lax.broadcasted_iota(jnp.int32, (B, 2 * B), 1)
    mean = jnp.where(c // 2 == r, 0.5, 0.0).astype(BF16)
    half = mean[:64, :128]
    for src, dst in ((q_ref, qc_ref), (k_ref, kc_ref), (v_ref, vc_ref)):
        for i in range(tokens // 256):
            dst[i * B:(i + 1) * B, :] = nn(mean, src[i * 256:(i + 1) * 256, :]).astype(BF16)
    for level in range(2, LOCAL + 1):
        before, here = offset(level - 1, tokens), offset(level, tokens)
        for dst in (qc_ref, kc_ref, vc_ref):
            for i in range((tokens >> level) // B):
                rows = dst[before + i * 256:before + (i + 1) * 256, :]
                dst[here + i * B:here + (i + 1) * B, :] = nn(mean, rows).astype(BF16)
    tail = offset(LOCAL + 1, tokens)
    for dst in (qc_ref, kc_ref, vc_ref):
        x5 = nn(half, dst[tail - B:tail, :]).astype(BF16)
        x6 = nn(half[:32, :64], x5).astype(BF16)
        x7 = nn(half[:16, :32], x6).astype(BF16)
        x8 = nn(half[:16, :16], x7).astype(BF16)
        dst[tail:tail + 64, :] = x5
        dst[tail + 64:tail + 96, :] = x6
        dst[tail + 96:tail + 112, :] = x7
        dst[tail + 112:tail + 128, :] = x8
    tail = tokens - 64
    for lane, src in ((0, kc_ref), (HD, vc_ref)):
        columns = slice(lane, lane + HD)
        m1_ref[:B, columns] = src[tokens - 256:tokens - 128, :]
        m2_ref[:64, columns] = src[tokens - 128:tail, :]
        m1_ref[B:, columns] = src[tail:, :]
        m2_ref[64:, columns] = src[tail:, :]


def coarsen(q, k, v):
    shape = jax.ShapeDtypeStruct(q.shape, BF16)
    tokens, width = q.shape
    sizes = (192, 128)
    return call(
        coarsen_kernel,
        6,
        grid=(width // HD,),
        in_specs=[spec(tokens)] * 3,
        out_specs=[spec(tokens)] * 3 + [both(n) for n in sizes],
        out_shape=[shape] * 3 + [jax.ShapeDtypeStruct((n, 2 * width), BF16) for n in sizes],
        name="coarsen",
    )(q, k, v)


def forward_blocks(blocks):
    scores = [nt(q, k) for q, k, _ in blocks]
    expos = [jnp.exp2(x * EXP_SCALE).astype(BF16) for x in scores]
    return [nn(e, with_ones(v)) for e, (_, _, v) in zip(expos, blocks)]


def sibling_pairs(level, tokens):
    off = offset(level, tokens)
    for i in range(0, tokens >> level, 256):
        lo, hi = (off + i, i), (off + i + B, i + B)
        yield lo, hi
        yield hi, lo


def local_forward_kernel(q_ref, k_ref, v_ref, qc_ref, kc_ref, vc_ref, numer_ref, total_ref, *scr):
    tokens = q_ref.shape[0]
    for levels in ((3, 2), (1,)):
        pairs = [(level, *pair) for level in levels for pair in sibling_pairs(level, tokens)]
        blocks = []
        for _, (ma, _), (oa, _) in pairs:
            mine, other = slice(ma, ma + B), slice(oa, oa + B)
            blocks.append((qc_ref[mine, :], kc_ref[other, :], vc_ref[other, :]))
        for (level, (_, at), _), u in zip(pairs, forward_blocks(blocks)):
            n, t = u[:, :HD], u[:, HD:]
            if level < LOCAL - 1:
                n = n + 2.0 * scr[2 * level][at:at + B, :]
                t = t + 2.0 * scr[2 * level + 1][at:at + B, :]
            repeat2(n, scr[2 * level - 2], 2 * at)
            repeat2(t, scr[2 * level - 1], 2 * at)
    for i in range(0, tokens, 1024):
        rows = [slice(at, at + 256) for at in range(i, i + 1024, 256)]
        sums = forward_blocks([(q_ref[r, :], k_ref[r, :], v_ref[r, :]) for r in rows])
        for r, u in zip(rows, sums):
            numer_ref[0, r, :] = u[:, :HD] + 2.0 * scr[0][r, :]
            total_ref[0, r, :] = u[:, HD:] + 2.0 * scr[1][r, :]


def local_forward(head, q, k, v, qc, kc, vc):
    tokens, width = q.shape
    scratch = []
    for level in range(1, LOCAL):
        scratch += [pltpu.VMEM((tokens >> (level - 1), HD), F32)] * 2
    columns = pl.BlockSpec((tokens, HD), lambda i: (0, head))
    return call(
        local_forward_kernel,
        5,
        grid=(1,),
        in_specs=[columns] * 6,
        out_specs=[lead(tokens, HD)] * 2,
        out_shape=[jax.ShapeDtypeStruct((1, tokens, HD), F32)] * 2,
        scratch_shapes=scratch,
        name="local_forward",
    )(q, k, v, qc, kc, vc)


def level_of_row(row):
    steps = [(row >= edge).astype(jnp.int32) for edge in (128, 192, 224, 240, 248)]
    return sum(steps)


KEYS = 640
ARRIVED = (192, 128, 128, 160, 96, 96, 128)
USED = (128, 64, 64, 128, 64, 64, 128)


def spread_levels(packed, scratch, weight):
    bounds = (0, 128, 192, 224, 240, 248)
    x = packed[240:248, :]
    for i in range(3, -1, -1):
        lo, hi = bounds[i], bounds[i + 1]
        repeat2(x, scratch)
        x = packed[lo:hi, :] + weight * scratch[0:hi - lo, :]
    return x


def repeat16(x):
    high = x.astype(BF16)
    low = (x - high.astype(F32)).astype(BF16)
    r = lax.broadcasted_iota(jnp.int32, (256, 32), 0)
    c = lax.broadcasted_iota(jnp.int32, (256, 32), 1)
    copies = jnp.where((r >> 4) == (c & 15), 1.0, 0.0).astype(BF16)
    for i in range(x.shape[0] // 16):
        part = slice(i * 16, i * 16 + 16)
        yield slice(i * 256, i * 256 + 256), nn(copies, jnp.concatenate([high[part], low[part]], axis=0))


def coarse_forward_kernel(numer0, total0, numer1, total1, q_ref, *refs):
    arrived, (att_ref, rtot_ref, side_ref, small) = refs[:7], refs[7:]
    at = 0
    for ref, n in zip(arrived, USED):
        side_ref[at:at + n, :] = ref[:n, :]
        at += n
    rows = q_ref.shape[0]
    level = level_of_row(lax.broadcasted_iota(jnp.int32, (rows, KEYS), 0))
    other = lax.broadcasted_iota(jnp.int32, (rows, KEYS), 1) // B
    expos = jnp.where(level == other, jnp.exp2(nt(q_ref[...], side_ref[:, :HD]) * EXP_SCALE), 0.0)
    u = nn(expos.astype(BF16), with_ones(side_ref[:, HD:]))
    parts = [16.0 * spread_levels(u[:, half], small, 2.0) for half in (slice(0, HD), slice(HD, None))]
    coarse = jnp.concatenate(parts, axis=1)
    for head, numer_ref, total_ref in ((0, numer0, total0), (1, numer1, total1)):

        @pl.when(pl.program_id(0) == head)
        def _():
            for at, x in repeat16(coarse):
                rtot = 1.0 / (total_ref[0, at, :] + x[:, HD:])
                rtot_ref[0, at, :] = rtot
                att_ref[at, :] = ((numer_ref[0, at, :] + x[:, :HD]) * rtot).astype(BF16)


def coarse_forward(local, qc, arrived):
    tokens, width = qc.shape
    heads = width // HD
    whole = pl.BlockSpec((1, tokens, HD), lambda h: (0, 0, 0))
    return call(
        coarse_forward_kernel,
        6,
        grid=(heads,),
        in_specs=[whole] * 4
        + [spec(256, tokens // 256 - 1)]
        + [both(n) for n in ARRIVED],
        out_specs=[spec(tokens), lead(tokens, HD), both(KEYS)],
        out_shape=[
            jax.ShapeDtypeStruct((tokens, heads * HD), BF16),
            jax.ShapeDtypeStruct((heads, tokens, HD), F32),
            jax.ShapeDtypeStruct((KEYS, 2 * heads * HD), BF16),
        ],
        scratch_shapes=[pltpu.VMEM((B, HD), F32)],
        name="coarse_forward",
    )(*local, qc, *arrived)


def with_dot(g, dot):
    lane = lax.broadcasted_iota(jnp.int32, dot.shape, 1)
    high = (-dot).astype(BF16)
    low = (-dot - high.astype(F32)).astype(BF16)
    zero = jnp.zeros(dot.shape, BF16)
    parts = jnp.where(lane == 0, high, jnp.where(lane == 1, low, zero))
    return jnp.concatenate([g.astype(BF16), parts], axis=1)


def backward_blocks(blocks, mask=None):
    scores = [nt(k, q) for q, k, _, _ in blocks]
    probes = [nt(with_ones(v), g) for _, _, v, g in blocks]
    expos = [jnp.exp2(x * EXP_SCALE) for x in scores]
    if mask is not None:
        expos = [jnp.where(mask, e, 0.0) for e in expos]
    slopes = [(e * p).astype(BF16) for e, p in zip(expos, probes)]
    dv = [nn(e.astype(BF16), g[:, :HD]) for e, (_, _, _, g) in zip(expos, blocks)]
    dk = [nn(s, q) for s, (q, _, _, _) in zip(slopes, blocks)]
    dq = [tn(s, k) for s, (_, k, _, _) in zip(slopes, blocks)]
    return list(zip(dq, dk, dv))


def coarse_backward_kernel(
    ga_ref, att_ref, rtot_ref, q_ref, side_ref, g0_ref, gc_ref, dq_ref, *refs
):
    sent, (g_scr, d_scr, small) = refs[:5], refs[5:]
    tokens = ga_ref.shape[0]
    step = 256
    for i in range(tokens // step):
        rows = slice(i * step, (i + 1) * step)
        ga = ga_ref[rows, :].astype(F32)
        rtot = rtot_ref[0, rows, :]
        g = ga * rtot
        dot = jnp.sum(ga * att_ref[rows, :].astype(F32), axis=1, keepdims=True) * rtot
        g_scr[rows, :] = g
        d_scr[rows, :] = dot
        g0_ref[0, rows, :] = with_dot(g, dot)
    for level in range(1, 9):
        n = tokens >> level
        here = offset(level, tokens)
        chunk = min(n, 256)
        for i in range(n // chunk):
            even, odd = pl.ds(2 * i * chunk, chunk, stride=2), pl.ds(2 * i * chunk + 1, chunk, stride=2)
            g = g_scr[even, :] + g_scr[odd, :]
            dot = d_scr[even, :] + d_scr[odd, :]
            g_scr[i * chunk:(i + 1) * chunk, :] = g
            d_scr[i * chunk:(i + 1) * chunk, :] = dot
            if n < 16:
                pad = jnp.zeros((16 - n, HD), F32)
                g, dot = jnp.concatenate([g, pad], axis=0), jnp.concatenate([dot, pad], axis=0)
            gc_ref[0, here + i * chunk:here + i * chunk + g.shape[0], :] = with_dot(g, dot)
    rows = q_ref.shape[0]
    level = level_of_row(lax.broadcasted_iota(jnp.int32, (KEYS, rows), 1))
    other = lax.broadcasted_iota(jnp.int32, (KEYS, rows), 0) // B
    g = gc_ref[0, tokens - rows:tokens, :]
    block = (q_ref[...], side_ref[:, :HD], side_ref[:, HD:], g)
    (dq, dk, dv), = backward_blocks([block], level == other)
    dq_ref[0] = spread_levels(dq, small, 1.0)
    for lane, d in ((0, (dk * SCALE).astype(BF16)), (HD, dv.astype(BF16))):
        for i, ref in enumerate(sent):
            ref[:, lane:lane + HD] = d[i * B:(i + 1) * B, :]


def coarse_backward(ga, att, rtot, qc, side):
    heads, tokens, _ = rtot.shape
    wide = jax.ShapeDtypeStruct((heads, tokens, 2 * HD), BF16)
    return call(
        coarse_backward_kernel,
        6,
        grid=(heads,),
        in_specs=[spec(tokens)] * 2 + [lead(tokens, HD), spec(256, tokens // 256 - 1), both(KEYS)],
        out_specs=[lead(tokens, 2 * HD)] * 2 + [lead(B, HD)] + [both(B)] * 5,
        out_shape=[wide, wide, jax.ShapeDtypeStruct((heads, B, HD), F32)]
        + [jax.ShapeDtypeStruct((B, 2 * heads * HD), BF16)] * 5,
        scratch_shapes=[pltpu.VMEM((tokens, HD), F32)] * 2 + [pltpu.VMEM((B, HD), F32)],
        name="coarse_backward",
    )(ga, att, rtot, qc, side)


SCRATCH = 3 * (LOCAL - 1) + 1


def local_backward_kernel(
    q_ref, k_ref, v_ref, qc_ref, kc_ref, vc_ref, g0_ref, gc_ref, dq4_ref, *refs
):
    (dq_ref, dk_ref, dv_ref), scr = refs[-SCRATCH - 3:-SCRATCH], refs[-SCRATCH:]
    tokens = q_ref.shape[0]
    repeat2(dq4_ref[0], scr[3 * (LOCAL - 1)])
    for levels in ((3, 2), (1,)):
        pairs = [(level, *pair) for level in levels for pair in sibling_pairs(level, tokens)]
        blocks = []
        for _, (ma, _), (oa, _) in pairs:
            mine, other = slice(ma, ma + B), slice(oa, oa + B)
            blocks.append((qc_ref[mine, :], kc_ref[other, :], vc_ref[other, :], gc_ref[0, mine, :]))
        for (level, (_, mr), (_, orow)), (dq, dk, dv) in zip(pairs, backward_blocks(blocks)):
            dq = dq + scr[3 * level][mr:mr + B, :]
            if level < LOCAL - 1:
                dk = dk + scr[3 * level + 1][orow:orow + B, :]
                dv = dv + scr[3 * level + 2][orow:orow + B, :]
            repeat2(dq, scr[3 * level - 3], 2 * mr)
            repeat2(dk, scr[3 * level - 2], 2 * orow)
            repeat2(dv, scr[3 * level - 1], 2 * orow)
    for i in range(0, tokens, 512):
        rows = [slice(at, at + 256) for at in range(i, i + 512, 256)]
        blocks = [(q_ref[r, :], k_ref[r, :], v_ref[r, :], g0_ref[0, r, :]) for r in rows]
        for r, (dq, dk, dv) in zip(rows, backward_blocks(blocks)):
            dq_ref[r, :] = ((dq + scr[0][r, :]) * SCALE).astype(BF16)
            dk_ref[r, :] = ((dk + scr[1][r, :]) * SCALE).astype(BF16)
            dv_ref[r, :] = (dv + scr[2][r, :]).astype(BF16)


def local_backward(head, inputs, before=()):
    tokens, width = inputs[0].shape
    scratch = []
    for level in range(1, LOCAL):
        scratch += [pltpu.VMEM((tokens >> (level - 1), HD), F32)] * 3
    scratch += [pltpu.VMEM((tokens >> (LOCAL - 1), HD), F32)]
    columns = pl.BlockSpec((tokens, HD), lambda i: (0, head))
    wide = pl.BlockSpec((1, tokens, 2 * HD), lambda i: (head, 0, 0))
    small = pl.BlockSpec((1, B, HD), lambda i: (head, 0, 0))
    return call(
        local_backward_kernel,
        8,
        grid=(1,),
        in_specs=[columns] * 6 + [wide] * 2 + [small] + [pl.BlockSpec(memory_space=pl.ANY)] * len(before),
        out_specs=[columns] * 3,
        out_shape=[jax.ShapeDtypeStruct((tokens, width), BF16)] * 3,
        scratch_shapes=scratch,
        input_output_aliases={9 + i: i for i in range(len(before))},
        name="local_backward",
    )(*inputs, *before)


def finish_kernel(dk_ref, dv_ref, own, across, r1, r2, r3, gk_ref, gv_ref, small):
    rows = lambda ref, lo, hi: ref[lo:hi, :].astype(F32)
    x4 = rows(r1, 0, 128)
    x5 = rows(r2, 0, 64) + rows(r3, 0, 64)
    own, across = rows(own, 0, 64), rows(across, 0, 32)
    packed = jnp.concatenate([x4, x5, own[:32], across[8:24], own[32:40] + across[24:]], axis=0)
    parts = [spread_levels(packed[:, half], small, 1.0) for half in (slice(0, HD), slice(HD, None))]
    for at, x in repeat16(jnp.concatenate(parts, axis=1)):
        gk_ref[at, :] = (dk_ref[at, :].astype(F32) + x[:, :HD]).astype(BF16)
        gv_ref[at, :] = (dv_ref[at, :].astype(F32) + x[:, HD:]).astype(BF16)


def finish(dk, dv, returned):
    tokens, width = dk.shape
    shape = jax.ShapeDtypeStruct((tokens, width), BF16)
    return call(
        finish_kernel,
        4,
        grid=(width // HD,),
        in_specs=[spec(tokens)] * 2 + [both(n) for n in (64, 32, 192, 128, 128)],
        out_specs=[spec(tokens)] * 2,
        out_shape=[shape] * 2,
        scratch_shapes=[pltpu.VMEM((B, HD), F32)],
        name="finish",
    )(dk, dv, *returned)


def mix_kernel(att_ref, w_ref, out_ref, held, sem):
    shards, _, width = att_ref.shape
    chunk = 512
    copies = []
    for c in range(out_ref.shape[1] // chunk):
        columns = pl.ds(c * chunk, chunk)
        copies.append(pltpu.make_async_copy(w_ref.at[:, columns], held.at[:, columns], sem.at[c]))
        copies[-1].start()
    att = jnp.concatenate([att_ref[j] for j in range(shards)], axis=1)
    for c, copy in enumerate(copies):
        columns = slice(c * chunk, (c + 1) * chunk)
        copy.wait()
        out_ref[:, columns] = nn(att, held[:, columns]).astype(BF16)


def mix(att, w):
    shards, rows, width = att.shape
    whole = pl.BlockSpec(memory_space=pltpu.VMEM)
    return call(
        mix_kernel,
        6,
        in_specs=[whole, pl.BlockSpec(memory_space=pl.ANY)],
        out_specs=whole,
        out_shape=jax.ShapeDtypeStruct((rows, w.shape[1]), BF16),
        scratch_shapes=[pltpu.VMEM(w.shape, BF16), pltpu.SemaphoreType.DMA((w.shape[1] // 512,))],
        name="mix",
    )(att, w)


def swap(x, axis, distance):
    return lax.ppermute(x, axis, [(i, i ^ distance) for i in range(lax.axis_size(axis))])


def shift_y(x, distance):
    n = lax.axis_size("seq")
    return lax.ppermute(x, "seq", [(i, (i + 8 * distance) % n) for i in range(n)])


def after(x, *others):
    return lax.optimization_barrier((x,) + others)[0]


def cat(parts):
    return jnp.concatenate(parts, axis=0)


def levels_of(x):
    n = x.shape[0]
    return x[n - 64:n - 32], x[n - 32:n - 16], x[n - 16:n - 8]


def add(*parts):
    return sum(x.astype(F32) for x in parts).astype(BF16)


def quarters(x, place):
    n = x.shape[1] // 4
    return [lax.dynamic_slice_in_dim(x, (place ^ j) * n, n, 1) for j in range(4)]


def join_quarters(parts, places):
    n = parts[0].shape[1]
    whole = jnp.concatenate([jnp.zeros(p.shape, p.dtype) for p in parts], 1)
    for place, part in zip(places, parts):
        whole = lax.dynamic_update_slice_in_dim(whole, part, place * n, 1)
    return whole


def body(queries, keys, values, w_out, grad_out):
    tokens, width = queries.shape
    shards = lax.axis_size("head")
    assert shards == 8 and lax.axis_size("seq") == 32
    y = lax.axis_index("seq") >> 3
    cotangent = lax.all_gather(grad_out, "head", axis=0, tiled=True)
    w_full = lax.all_gather(w_out, "head", axis=0, tiled=True)

    qc, kc, vc, m1, m2 = coarsen(queries, keys, values)
    near = [swap(m1, "seq", 1), swap(m2, "seq", 2), swap(m2, "seq", 3)]
    inputs = (queries, keys, values, qc, kc)
    local = tuple(local_forward(0, *inputs, vc))
    near = after(tuple(near), local[0])
    six, seven, eight = (cat(parts) for parts in zip(*[levels_of(x) for x in (m1, *near)]))
    group = cat([seven, eight])
    far = [swap(cat([six, eight]), "seq", 7), swap(group, "seq", 8), swap(group, "seq", 15)]
    local += tuple(local_forward(1, *inputs, after(vc, six)))
    far = after(tuple(far), local[2])
    last = swap(cat([eight] + [x[x.shape[0] - 32:] for x in far]), "seq", 24)
    attended, rtot, side = coarse_forward(local, qc, (*near, *far, last))

    mine = lax.all_to_all(attended.reshape(shards, tokens // shards, width), "head", 0, 0)
    grad_weight = tn(attended, cotangent).astype(BF16)
    ga = nt(cotangent, after(w_out, grad_weight)).astype(BF16)
    own, *rest = quarters(grad_weight, y)
    rest = [swap(x, "seq", 8 * (j + 1)) for j, x in enumerate(rest)]
    g0, gc, dq4, e4, e5, e6, e7, e8 = coarse_backward(ga, attended, rtot, qc, side)
    rest = after(tuple(rest), dq4)
    partial = add(own, *rest)
    mine = after(mine, dq4)

    x8 = swap(after(e8, mine), "seq", 24)
    low = swap(partial, "seq", 1)
    inputs = (queries, keys, values, qc, kc, vc, g0, gc)
    done = local_backward(0, inputs + (after(dq4, partial),))
    low, x8 = after((low, x8), done[0])
    partial = add(partial, low)

    f7 = swap(cat([e6, e7[64:], x8[32:64], x8[96:]]), "seq", 7)
    low = swap(partial, "seq", 3)
    grad_q, dk, dv = local_backward(1, inputs + (after(dq4, partial, x8),), done)
    low, f7 = after((low, f7), grad_q)
    partial = add(partial, low)

    x6, x7 = f7[:B], add(e7[:64], f7[128:192])
    here, there = add(x8[:32], f7[192:224]), add(x8[64:96], f7[224:])
    first = [e4, e5[:64], e5[64:]]
    tails = []
    for j in range(4):
        tails.append(cat([x6[32 * j:][:32], here[8 * j:][:8], x7[16 * j:][:16], there[8 * j:][:8]]))
    near = [swap(cat([x, tails[j + 1]]), "seq", j + 1) for j, x in enumerate(first)]
    low = swap(partial, "seq", 7)
    mixed = mix(after(mine, partial, tails[0]), w_full)
    near, low = after((near, low), mixed)
    summed = add(partial, low)

    tail = add(tails[0], *[x[x.shape[0] - 64:] for x in near])
    across = swap(tail[32:], "seq", 8)
    up, down = shift_y(summed, 1), shift_y(summed, -1)
    up, down, across = after((up, down, across), summed)
    far = cat([shift_y(up[:B], 1), shift_y(down[B:], -1)])
    grad_k, grad_v = finish(after(dk, up, down), dv, (tail, across, *near))
    far = after(far, grad_k)
    places = [y, (y + 3) & 3, (y + 1) & 3, (y + 2) & 3]
    return mixed, grad_q, grad_k, grad_v, join_quarters([summed, up, down, far], places)


def solution(mesh):
    return jax.shard_map(
        body,
        mesh=mesh,
        in_specs=(
            P("seq", "head"),
            P("seq", "head"),
            P("seq", "head"),
            P("head", None),
            P(("seq", "head"), None),
        ),
        out_specs=(
            P(("seq", "head"), None),
            P("seq", "head"),
            P("seq", "head"),
            P("seq", "head"),
            P("head", None),
        ),
        check_vma=False,
    )
```

```python
import functools
import jax
import jax.numpy as jnp
from jax import lax
from jax.experimental import pallas as pl
from jax.experimental.pallas import tpu as pltpu
from jax.sharding import PartitionSpec as P

HD = 128
B = 128
LOCAL = 4
F32 = jnp.float32
BF16 = jnp.bfloat16
EXP_SCALE = 1.4426950408889634 * HD ** (-0.5)
SCALE = HD ** (-0.5)
VMEM = 56 * 1024 * 1024
COST = 0.05e6


def nn(a, b):
    return lax.dot_general(a, b, (((1,), (0,)), ((), ())), preferred_element_type=F32)


def nt(a, b):
    return lax.dot_general(a, b, (((1,), (1,)), ((), ())), preferred_element_type=F32)


def tn(a, b):
    return lax.dot_general(a, b, (((0,), (0,)), ((), ())), preferred_element_type=F32)


def call(kernel, micros, **kwargs):
    cost = pl.CostEstimate(flops=0, bytes_accessed=int(micros * COST), transcendentals=0)
    return pl.pallas_call(
        kernel,
        cost_estimate=cost,
        compiler_params=pltpu.CompilerParams(vmem_limit_bytes=VMEM),
        **kwargs,
    )


def offset(level, tokens):
    return tokens - (tokens >> (level - 1))


def spec(rows, block=0):
    return pl.BlockSpec((rows, HD), lambda h: (block, h))


def lead(rows, width):
    return pl.BlockSpec((1, rows, width), lambda h: (h, 0, 0))


def both(rows):
    return pl.BlockSpec((rows, 2 * HD), lambda h: (0, h))


def with_ones(v):
    return jnp.concatenate([v, jnp.ones(v.shape, BF16)], axis=1)


def repeat2(x, scratch, base=0):
    n = x.shape[0]
    scratch[pl.ds(base, n, stride=2), :] = x
    scratch[pl.ds(base + 1, n, stride=2), :] = x


def coarsen_kernel(q_ref, k_ref, v_ref, qc_ref, kc_ref, vc_ref, m1_ref, m2_ref):
    tokens = q_ref.shape[0]
    r = lax.broadcasted_iota(jnp.int32, (B, 2 * B), 0)
    c = lax.broadcasted_iota(jnp.int32, (B, 2 * B), 1)
    mean = jnp.where(c // 2 == r, 0.5, 0.0).astype(BF16)
    half = mean[:64, :128]
    for src, dst in ((q_ref, qc_ref), (k_ref, kc_ref), (v_ref, vc_ref)):
        for i in range(tokens // 256):
            dst[i * B:(i + 1) * B, :] = nn(mean, src[i * 256:(i + 1) * 256, :]).astype(BF16)
    for level in range(2, LOCAL + 1):
        before, here = offset(level - 1, tokens), offset(level, tokens)
        for dst in (qc_ref, kc_ref, vc_ref):
            for i in range((tokens >> level) // B):
                rows = dst[before + i * 256:before + (i + 1) * 256, :]
                dst[here + i * B:here + (i + 1) * B, :] = nn(mean, rows).astype(BF16)
    tail = offset(LOCAL + 1, tokens)
    for dst in (qc_ref, kc_ref, vc_ref):
        x5 = nn(half, dst[tail - B:tail, :]).astype(BF16)
        x6 = nn(half[:32, :64], x5).astype(BF16)
        x7 = nn(half[:16, :32], x6).astype(BF16)
        x8 = nn(half[:16, :16], x7).astype(BF16)
        dst[tail:tail + 64, :] = x5
        dst[tail + 64:tail + 96, :] = x6
        dst[tail + 96:tail + 112, :] = x7
        dst[tail + 112:tail + 128, :] = x8
    tail = tokens - 64
    for lane, src in ((0, kc_ref), (HD, vc_ref)):
        columns = slice(lane, lane + HD)
        m1_ref[:B, columns] = src[tokens - 256:tokens - 128, :]
        m2_ref[:64, columns] = src[tokens - 128:tail, :]
        m1_ref[B:, columns] = src[tail:, :]
        m2_ref[64:, columns] = src[tail:, :]


def coarsen(q, k, v):
    shape = jax.ShapeDtypeStruct(q.shape, BF16)
    tokens, width = q.shape
    sizes = (192, 128)
    return call(
        coarsen_kernel,
        6,
        grid=(width // HD,),
        in_specs=[spec(tokens)] * 3,
        out_specs=[spec(tokens)] * 3 + [both(n) for n in sizes],
        out_shape=[shape] * 3 + [jax.ShapeDtypeStruct((n, 2 * width), BF16) for n in sizes],
        name="coarsen",
    )(q, k, v)


def forward_blocks(blocks):
    scores = [nt(q, k) for q, k, _ in blocks]
    expos = [jnp.exp2(x * EXP_SCALE).astype(BF16) for x in scores]
    return [nn(e, with_ones(v)) for e, (_, _, v) in zip(expos, blocks)]


def sibling_pairs(level, tokens):
    off = offset(level, tokens)
    for i in range(0, tokens >> level, 256):
        lo, hi = (off + i, i), (off + i + B, i + B)
        yield lo, hi
        yield hi, lo


def local_forward_kernel(q_ref, k_ref, v_ref, qc_ref, kc_ref, vc_ref, numer_ref, total_ref, *scr):
    tokens = q_ref.shape[0]
    for levels in ((3, 2), (1,)):
        pairs = [(level, *pair) for level in levels for pair in sibling_pairs(level, tokens)]
        blocks = []
        for _, (ma, _), (oa, _) in pairs:
            mine, other = slice(ma, ma + B), slice(oa, oa + B)
            blocks.append((qc_ref[mine, :], kc_ref[other, :], vc_ref[other, :]))
        for (level, (_, at), _), u in zip(pairs, forward_blocks(blocks)):
            n, t = u[:, :HD], u[:, HD:]
            if level < LOCAL - 1:
                n = n + 2.0 * scr[2 * level][at:at + B, :]
                t = t + 2.0 * scr[2 * level + 1][at:at + B, :]
            repeat2(n, scr[2 * level - 2], 2 * at)
            repeat2(t, scr[2 * level - 1], 2 * at)
    for i in range(0, tokens, 1024):
        rows = [slice(at, at + 256) for at in range(i, i + 1024, 256)]
        sums = forward_blocks([(q_ref[r, :], k_ref[r, :], v_ref[r, :]) for r in rows])
        for r, u in zip(rows, sums):
            numer_ref[0, r, :] = u[:, :HD] + 2.0 * scr[0][r, :]
            total_ref[0, r, :] = u[:, HD:] + 2.0 * scr[1][r, :]


def local_forward(head, q, k, v, qc, kc, vc):
    tokens, width = q.shape
    scratch = []
    for level in range(1, LOCAL):
        scratch += [pltpu.VMEM((tokens >> (level - 1), HD), F32)] * 2
    columns = pl.BlockSpec((tokens, HD), lambda i: (0, head))
    return call(
        local_forward_kernel,
        5,
        grid=(1,),
        in_specs=[columns] * 6,
        out_specs=[lead(tokens, HD)] * 2,
        out_shape=[jax.ShapeDtypeStruct((1, tokens, HD), F32)] * 2,
        scratch_shapes=scratch,
        name="local_forward",
    )(q, k, v, qc, kc, vc)


def level_of_row(row):
    steps = [(row >= edge).astype(jnp.int32) for edge in (128, 192, 224, 240, 248)]
    return sum(steps)


KEYS = 640
ARRIVED = (192, 128, 128, 160, 96, 96, 128)
USED = (128, 64, 64, 128, 64, 64, 128)


def spread_levels(packed, scratch, weight):
    bounds = (0, 128, 192, 224, 240, 248)
    x = packed[240:248, :]
    for i in range(3, -1, -1):
        lo, hi = bounds[i], bounds[i + 1]
        repeat2(x, scratch)
        x = packed[lo:hi, :] + weight * scratch[0:hi - lo, :]
    return x


def repeat16(x):
    high = x.astype(BF16)
    low = (x - high.astype(F32)).astype(BF16)
    r = lax.broadcasted_iota(jnp.int32, (256, 32), 0)
    c = lax.broadcasted_iota(jnp.int32, (256, 32), 1)
    copies = jnp.where((r >> 4) == (c & 15), 1.0, 0.0).astype(BF16)
    for i in range(x.shape[0] // 16):
        part = slice(i * 16, i * 16 + 16)
        yield slice(i * 256, i * 256 + 256), nn(copies, jnp.concatenate([high[part], low[part]], axis=0))


def coarse_forward_kernel(numer0, total0, numer1, total1, q_ref, *refs):
    arrived, (att_ref, rtot_ref, side_ref, small) = refs[:7], refs[7:]
    at = 0
    for ref, n in zip(arrived, USED):
        side_ref[at:at + n, :] = ref[:n, :]
        at += n
    rows = q_ref.shape[0]
    level = level_of_row(lax.broadcasted_iota(jnp.int32, (rows, KEYS), 0))
    other = lax.broadcasted_iota(jnp.int32, (rows, KEYS), 1) // B
    expos = jnp.where(level == other, jnp.exp2(nt(q_ref[...], side_ref[:, :HD]) * EXP_SCALE), 0.0)
    u = nn(expos.astype(BF16), with_ones(side_ref[:, HD:]))
    parts = [16.0 * spread_levels(u[:, half], small, 2.0) for half in (slice(0, HD), slice(HD, None))]
    coarse = jnp.concatenate(parts, axis=1)
    for head, numer_ref, total_ref in ((0, numer0, total0), (1, numer1, total1)):

        @pl.when(pl.program_id(0) == head)
        def _():
            for at, x in repeat16(coarse):
                rtot = 1.0 / (total_ref[0, at, :] + x[:, HD:])
                rtot_ref[0, at, :] = rtot
                att_ref[at, :] = ((numer_ref[0, at, :] + x[:, :HD]) * rtot).astype(BF16)


def coarse_forward(local, qc, arrived):
    tokens, width = qc.shape
    heads = width // HD
    whole = pl.BlockSpec((1, tokens, HD), lambda h: (0, 0, 0))
    return call(
        coarse_forward_kernel,
        6,
        grid=(heads,),
        in_specs=[whole] * 4
        + [spec(256, tokens // 256 - 1)]
        + [both(n) for n in ARRIVED],
        out_specs=[spec(tokens), lead(tokens, HD), both(KEYS)],
        out_shape=[
            jax.ShapeDtypeStruct((tokens, heads * HD), BF16),
            jax.ShapeDtypeStruct((heads, tokens, HD), F32),
            jax.ShapeDtypeStruct((KEYS, 2 * heads * HD), BF16),
        ],
        scratch_shapes=[pltpu.VMEM((B, HD), F32)],
        name="coarse_forward",
    )(*local, qc, *arrived)


def with_dot(g, dot):
    lane = lax.broadcasted_iota(jnp.int32, dot.shape, 1)
    high = (-dot).astype(BF16)
    low = (-dot - high.astype(F32)).astype(BF16)
    zero = jnp.zeros(dot.shape, BF16)
    parts = jnp.where(lane == 0, high, jnp.where(lane == 1, low, zero))
    return jnp.concatenate([g.astype(BF16), parts], axis=1)


def backward_blocks(blocks, mask=None):
    scores = [nt(k, q) for q, k, _, _ in blocks]
    probes = [nt(with_ones(v), g) for _, _, v, g in blocks]
    expos = [jnp.exp2(x * EXP_SCALE) for x in scores]
    if mask is not None:
        expos = [jnp.where(mask, e, 0.0) for e in expos]
    slopes = [(e * p).astype(BF16) for e, p in zip(expos, probes)]
    dv = [nn(e.astype(BF16), g[:, :HD]) for e, (_, _, _, g) in zip(expos, blocks)]
    dk = [nn(s, q) for s, (q, _, _, _) in zip(slopes, blocks)]
    dq = [tn(s, k) for s, (_, k, _, _) in zip(slopes, blocks)]
    return list(zip(dq, dk, dv))


def coarse_backward_kernel(
    ga_ref, att_ref, rtot_ref, q_ref, side_ref, g0_ref, gc_ref, dq_ref, *refs
):
    sent, (g_scr, d_scr, small) = refs[:5], refs[5:]
    tokens = ga_ref.shape[0]
    step = 256
    for i in range(tokens // step):
        rows = slice(i * step, (i + 1) * step)
        ga = ga_ref[rows, :].astype(F32)
        rtot = rtot_ref[0, rows, :]
        g = ga * rtot
        dot = jnp.sum(ga * att_ref[rows, :].astype(F32), axis=1, keepdims=True) * rtot
        g_scr[rows, :] = g
        d_scr[rows, :] = dot
        g0_ref[0, rows, :] = with_dot(g, dot)
    for level in range(1, 9):
        n = tokens >> level
        here = offset(level, tokens)
        chunk = min(n, 256)
        for i in range(n // chunk):
            even, odd = pl.ds(2 * i * chunk, chunk, stride=2), pl.ds(2 * i * chunk + 1, chunk, stride=2)
            g = g_scr[even, :] + g_scr[odd, :]
            dot = d_scr[even, :] + d_scr[odd, :]
            g_scr[i * chunk:(i + 1) * chunk, :] = g
            d_scr[i * chunk:(i + 1) * chunk, :] = dot
            if n < 16:
                pad = jnp.zeros((16 - n, HD), F32)
                g, dot = jnp.concatenate([g, pad], axis=0), jnp.concatenate([dot, pad], axis=0)
            gc_ref[0, here + i * chunk:here + i * chunk + g.shape[0], :] = with_dot(g, dot)
    rows = q_ref.shape[0]
    level = level_of_row(lax.broadcasted_iota(jnp.int32, (KEYS, rows), 1))
    other = lax.broadcasted_iota(jnp.int32, (KEYS, rows), 0) // B
    g = gc_ref[0, tokens - rows:tokens, :]
    block = (q_ref[...], side_ref[:, :HD], side_ref[:, HD:], g)
    (dq, dk, dv), = backward_blocks([block], level == other)
    dq_ref[0] = spread_levels(dq, small, 1.0)
    for lane, d in ((0, (dk * SCALE).astype(BF16)), (HD, dv.astype(BF16))):
        for i, ref in enumerate(sent):
            ref[:, lane:lane + HD] = d[i * B:(i + 1) * B, :]


def coarse_backward(ga, att, rtot, qc, side):
    heads, tokens, _ = rtot.shape
    wide = jax.ShapeDtypeStruct((heads, tokens, 2 * HD), BF16)
    return call(
        coarse_backward_kernel,
        6,
        grid=(heads,),
        in_specs=[spec(tokens)] * 2 + [lead(tokens, HD), spec(256, tokens // 256 - 1), both(KEYS)],
        out_specs=[lead(tokens, 2 * HD)] * 2 + [lead(B, HD)] + [both(B)] * 5,
        out_shape=[wide, wide, jax.ShapeDtypeStruct((heads, B, HD), F32)]
        + [jax.ShapeDtypeStruct((B, 2 * heads * HD), BF16)] * 5,
        scratch_shapes=[pltpu.VMEM((tokens, HD), F32)] * 2 + [pltpu.VMEM((B, HD), F32)],
        name="coarse_backward",
    )(ga, att, rtot, qc, side)


SCRATCH = 3 * (LOCAL - 1) + 1


def local_backward_kernel(
    q_ref, k_ref, v_ref, qc_ref, kc_ref, vc_ref, g0_ref, gc_ref, dq4_ref, *refs
):
    (dq_ref, dk_ref, dv_ref), scr = refs[-SCRATCH - 3:-SCRATCH], refs[-SCRATCH:]
    tokens = q_ref.shape[0]
    repeat2(dq4_ref[0], scr[3 * (LOCAL - 1)])
    for levels in ((3, 2), (1,)):
        pairs = [(level, *pair) for level in levels for pair in sibling_pairs(level, tokens)]
        blocks = []
        for _, (ma, _), (oa, _) in pairs:
            mine, other = slice(ma, ma + B), slice(oa, oa + B)
            blocks.append((qc_ref[mine, :], kc_ref[other, :], vc_ref[other, :], gc_ref[0, mine, :]))
        for (level, (_, mr), (_, orow)), (dq, dk, dv) in zip(pairs, backward_blocks(blocks)):
            dq = dq + scr[3 * level][mr:mr + B, :]
            if level < LOCAL - 1:
                dk = dk + scr[3 * level + 1][orow:orow + B, :]
                dv = dv + scr[3 * level + 2][orow:orow + B, :]
            repeat2(dq, scr[3 * level - 3], 2 * mr)
            repeat2(dk, scr[3 * level - 2], 2 * orow)
            repeat2(dv, scr[3 * level - 1], 2 * orow)
    for i in range(0, tokens, 512):
        rows = [slice(at, at + 256) for at in range(i, i + 512, 256)]
        blocks = [(q_ref[r, :], k_ref[r, :], v_ref[r, :], g0_ref[0, r, :]) for r in rows]
        for r, (dq, dk, dv) in zip(rows, backward_blocks(blocks)):
            dq_ref[r, :] = ((dq + scr[0][r, :]) * SCALE).astype(BF16)
            dk_ref[r, :] = ((dk + scr[1][r, :]) * SCALE).astype(BF16)
            dv_ref[r, :] = (dv + scr[2][r, :]).astype(BF16)


def local_backward(head, inputs, before=()):
    tokens, width = inputs[0].shape
    scratch = []
    for level in range(1, LOCAL):
        scratch += [pltpu.VMEM((tokens >> (level - 1), HD), F32)] * 3
    scratch += [pltpu.VMEM((tokens >> (LOCAL - 1), HD), F32)]
    columns = pl.BlockSpec((tokens, HD), lambda i: (0, head))
    wide = pl.BlockSpec((1, tokens, 2 * HD), lambda i: (head, 0, 0))
    small = pl.BlockSpec((1, B, HD), lambda i: (head, 0, 0))
    return call(
        local_backward_kernel,
        8,
        grid=(1,),
        in_specs=[columns] * 6 + [wide] * 2 + [small] + [pl.BlockSpec(memory_space=pl.ANY)] * len(before),
        out_specs=[columns] * 3,
        out_shape=[jax.ShapeDtypeStruct((tokens, width), BF16)] * 3,
        scratch_shapes=scratch,
        input_output_aliases={9 + i: i for i in range(len(before))},
        name="local_backward",
    )(*inputs, *before)


def finish_kernel(dk_ref, dv_ref, own, across, r1, r2, r3, gk_ref, gv_ref, small):
    rows = lambda ref, lo, hi: ref[lo:hi, :].astype(F32)
    x4 = rows(r1, 0, 128)
    x5 = rows(r2, 0, 64) + rows(r3, 0, 64)
    own, across = rows(own, 0, 64), rows(across, 0, 32)
    packed = jnp.concatenate([x4, x5, own[:32], across[8:24], own[32:40] + across[24:]], axis=0)
    parts = [spread_levels(packed[:, half], small, 1.0) for half in (slice(0, HD), slice(HD, None))]
    for at, x in repeat16(jnp.concatenate(parts, axis=1)):
        gk_ref[at, :] = (dk_ref[at, :].astype(F32) + x[:, :HD]).astype(BF16)
        gv_ref[at, :] = (dv_ref[at, :].astype(F32) + x[:, HD:]).astype(BF16)


def finish(dk, dv, returned):
    tokens, width = dk.shape
    shape = jax.ShapeDtypeStruct((tokens, width), BF16)
    return call(
        finish_kernel,
        4,
        grid=(width // HD,),
        in_specs=[spec(tokens)] * 2 + [both(n) for n in (64, 32, 192, 128, 128)],
        out_specs=[spec(tokens)] * 2,
        out_shape=[shape] * 2,
        scratch_shapes=[pltpu.VMEM((B, HD), F32)],
        name="finish",
    )(dk, dv, *returned)


def mix_kernel(att_ref, w_ref, out_ref, held, sem):
    shards, _, width = att_ref.shape
    chunk = 512
    copies = []
    for c in range(out_ref.shape[1] // chunk):
        columns = pl.ds(c * chunk, chunk)
        copies.append(pltpu.make_async_copy(w_ref.at[:, columns], held.at[:, columns], sem.at[c]))
        copies[-1].start()
    att = jnp.concatenate([att_ref[j] for j in range(shards)], axis=1)
    for c, copy in enumerate(copies):
        columns = slice(c * chunk, (c + 1) * chunk)
        copy.wait()
        out_ref[:, columns] = nn(att, held[:, columns]).astype(BF16)


def mix(att, w):
    shards, rows, width = att.shape
    whole = pl.BlockSpec(memory_space=pltpu.VMEM)
    return call(
        mix_kernel,
        6,
        in_specs=[whole, pl.BlockSpec(memory_space=pl.ANY)],
        out_specs=whole,
        out_shape=jax.ShapeDtypeStruct((rows, w.shape[1]), BF16),
        scratch_shapes=[pltpu.VMEM(w.shape, BF16), pltpu.SemaphoreType.DMA((w.shape[1] // 512,))],
        name="mix",
    )(att, w)


def swap(x, axis, distance):
    return lax.ppermute(x, axis, [(i, i ^ distance) for i in range(lax.axis_size(axis))])


def shift_y(x, distance):
    n = lax.axis_size("seq")
    return lax.ppermute(x, "seq", [(i, (i + 8 * distance) % n) for i in range(n)])


def after(x, *others):
    return lax.optimization_barrier((x,) + others)[0]


def cat(parts):
    return jnp.concatenate(parts, axis=0)


def levels_of(x):
    n = x.shape[0]
    return x[n - 64:n - 32], x[n - 32:n - 16], x[n - 16:n - 8]


def add(*parts):
    return sum(x.astype(F32) for x in parts).astype(BF16)


def quarters(x, place):
    n = x.shape[1] // 4
    return [lax.dynamic_slice_in_dim(x, (place ^ j) * n, n, 1) for j in range(4)]


def join_quarters(parts, places):
    n = parts[0].shape[1]
    whole = jnp.concatenate([jnp.zeros(p.shape, p.dtype) for p in parts], 1)
    for place, part in zip(places, parts):
        whole = lax.dynamic_update_slice_in_dim(whole, part, place * n, 1)
    return whole


def body(queries, keys, values, w_out, grad_out):
    tokens, width = queries.shape
    shards = lax.axis_size("head")
    assert shards == 8 and lax.axis_size("seq") == 32
    y = lax.axis_index("seq") >> 3
    cotangent = lax.all_gather(grad_out, "head", axis=0, tiled=True)
    w_full = lax.all_gather(w_out, "head", axis=0, tiled=True)

    qc, kc, vc, m1, m2 = coarsen(queries, keys, values)
    near = [swap(m1, "seq", 1), swap(m2, "seq", 2), swap(m2, "seq", 3)]
    inputs = (queries, keys, values, qc, kc)
    local = tuple(local_forward(0, *inputs, vc))
    near = after(tuple(near), local[0])
    six, seven, eight = (cat(parts) for parts in zip(*[levels_of(x) for x in (m1, *near)]))
    group = cat([seven, eight])
    far = [swap(cat([six, eight]), "seq", 7), swap(group, "seq", 8), swap(group, "seq", 15)]
    local += tuple(local_forward(1, *inputs, after(vc, six)))
    far = after(tuple(far), local[2])
    last = swap(cat([eight] + [x[x.shape[0] - 32:] for x in far]), "seq", 24)
    attended, rtot, side = coarse_forward(local, qc, (*near, *far, last))

    mine = lax.all_to_all(attended.reshape(shards, tokens // shards, width), "head", 0, 0)
    grad_weight = tn(attended, cotangent).astype(BF16)
    ga = nt(cotangent, after(w_out, grad_weight)).astype(BF16)
    own, *rest = quarters(grad_weight, y)
    rest = [swap(x, "seq", 8 * (j + 1)) for j, x in enumerate(rest)]
    g0, gc, dq4, e4, e5, e6, e7, e8 = coarse_backward(ga, attended, rtot, qc, side)
    rest = after(tuple(rest), dq4)
    partial = add(own, *rest)
    mine = after(mine, dq4)

    x8 = swap(after(e8, mine), "seq", 24)
    low = swap(partial, "seq", 3)
    inputs = (queries, keys, values, qc, kc, vc, g0, gc)
    done = local_backward(0, inputs + (after(dq4, partial),))
    low, x8 = after((low, x8), done[0])
    partial = add(partial, low)

    f7 = swap(cat([e6, e7[64:], x8[32:64], x8[96:]]), "seq", 7)
    low = swap(partial, "seq", 1)
    grad_q, dk, dv = local_backward(1, inputs + (after(dq4, partial, x8),), done)
    low, f7 = after((low, f7), grad_q)
    partial = add(partial, low)

    x6, x7 = f7[:B], add(e7[:64], f7[128:192])
    here, there = add(x8[:32], f7[192:224]), add(x8[64:96], f7[224:])
    first = [e4, e5[:64], e5[64:]]
    tails = []
    for j in range(4):
        tails.append(cat([x6[32 * j:][:32], here[8 * j:][:8], x7[16 * j:][:16], there[8 * j:][:8]]))
    near = [swap(cat([x, tails[j + 1]]), "seq", j + 1) for j, x in enumerate(first)]
    low = swap(partial, "seq", 7)
    mixed = mix(after(mine, partial, tails[0]), w_full)
    near, low = after((near, low), mixed)
    summed = add(partial, low)

    tail = add(tails[0], *[x[x.shape[0] - 64:] for x in near])
    across = swap(tail[32:], "seq", 8)
    up, down = shift_y(summed, 1), shift_y(summed, -1)
    up, down, across = after((up, down, across), summed)
    far = cat([shift_y(up[:B], 1), shift_y(down[B:], -1)])
    grad_k, grad_v = finish(after(dk, up, down), dv, (tail, across, *near))
    far = after(far, grad_k)
    places = [y, (y + 3) & 3, (y + 1) & 3, (y + 2) & 3]
    return mixed, grad_q, grad_k, grad_v, join_quarters([summed, up, down, far], places)


def solution(mesh):
    return jax.shard_map(
        body,
        mesh=mesh,
        in_specs=(
            P("seq", "head"),
            P("seq", "head"),
            P("seq", "head"),
            P("head", None),
            P(("seq", "head"), None),
        ),
        out_specs=(
            P(("seq", "head"), None),
            P("seq", "head"),
            P("seq", "head"),
            P("seq", "head"),
            P("head", None),
        ),
        check_vma=False,
    )
```
